32 devices in a mesh: patch: 4 (over y, core), map: 8 (over z, x).
Axes of the slice: x: 2, y: 2, z: 4, core: 2. Of those that a mesh axis runs over, the one named last changes fastest.
Arguments:
- maps: bfloat16 [16, 32, 6144], P('map', None, 'patch'), may hold values from -6 to 6
- cotangent: bfloat16 [16, 32, 6144], P('map', None, 'patch'), may hold values from -6 to 6
- tiles: bfloat16 [24, 3, 256, 256], P('patch'), may hold values from -0.21875 to 0.21875
- columns: int32 [24, 3], P('patch'), may hold values from 0 to 23, as said below
- filters: bfloat16 [3, 32, 32], replicated, may hold values from -0.625 to 0.625
Outputs:
- output: bfloat16 [16, 32, 6144], P('map', None, 'patch')
- input_grad: bfloat16 [16, 32, 6144], P('map', None, 'patch')
- filter_grad: float32 [3, 32, 32], replicated
The draws below stay inside these ranges and needn't reach their ends.
Inputs may be any that keep to these rules, and one draw needn't show every extreme that they name: `columns`: slot 0 of block row b names block b itself, slot 1 a block 1 to 2 before it and slot 2 a block 1 to 2 after it, counted cyclically over the 24 blocks; block row 0 reads exactly 2 blocks away on both sides.
All inputs are finite; a program needn't handle non-finite values.
Results may differ from the reference program's by a relative error of at most 0.0054.
Values may be sent and summed in bfloat16 or wider, within the bound.
A program may use at most 64 MiB of HBM per device.

```python
import math
import jax
import jax.numpy as jnp
from jax import lax

C = 32
ORDER = 3
BS = 256
SLOTS = 3
REACH = 2
MAP_DEV = 2
NBLK = 24
NPIX = 6144
MAPS = 16
N_MAP = 8


def draw_columns(key, part):
    left_key = jax.random.fold_in(key, 11)
    right_key = jax.random.fold_in(key, 23)
    block_ids = jnp.arange(NBLK, dtype=jnp.int32)
    back_step = jax.random.randint(left_key, (NBLK,), 1, REACH + 1, dtype=jnp.int32)
    next_step = jax.random.randint(right_key, (NBLK,), 1, REACH + 1, dtype=jnp.int32)
    back_step = back_step.at[0].set(REACH)
    next_step = next_step.at[0].set(REACH)
    return jnp.stack([block_ids, (block_ids - back_step) % NBLK, (block_ids + next_step) % NBLK], axis=1)


def block_scale(rng, dims, split, least, high):
    def one(dim, blocks):
        heights = jax.random.uniform(jax.random.fold_in(jax.random.fold_in(rng, 6), dim), (blocks,), jnp.float32, least / len(split), high / len(split))
        return jnp.repeat(jnp.exp(heights), dims[dim] // blocks).reshape((-1,) + (1,) * (len(dims) - dim - 1))

    level = one(*split[0])
    for cut in split[1:]:
        level = level * one(*cut)
    return level


def bell_draw(key, extent, scale, reach, cuts=(), held_as=jnp.bfloat16):
    values = scale * jax.random.normal(key, extent, jnp.float32)
    if cuts:
        values = values * block_scale(key, extent, cuts, -0.22, 0.18)
    return jnp.clip(values, -reach, reach).astype(held_as)


def setup_inputs(seed: int = 0) -> dict:
    seeds = jax.random.split(jax.random.key(seed), 6)
    maps = bell_draw(seeds[0], (MAPS, C, NPIX), 1.0, 6.0, ((0, 8), (2, 4)))
    cotangent = bell_draw(seeds[1], (MAPS, C, NPIX), 1.0, 6.0, ((0, 8), (2, 4)))
    tiles = bell_draw(seeds[2], (NBLK, SLOTS, BS, BS), (SLOTS * BS) ** -0.5, 0.21875, ((0, 4),))
    columns = draw_columns(jax.random.fold_in(seeds[5], 71), 0)
    filters = bell_draw(seeds[4], (ORDER, C, C), (ORDER * C) ** -0.5, 0.625)
    return dict(maps=maps, cotangent=cotangent, tiles=tiles, columns=columns, filters=filters)


def forward_apply(field, tiles_f, columns, block_count, block_size):
    ext_blocks = field.reshape(field.shape[0], block_count, block_size)
    picked = ext_blocks[:, columns]
    result = jnp.einsum('nbjq,bjiq->nbi', picked, tiles_f)
    return result.reshape(field.shape[0], block_count * block_size)

def adjoint_apply(field, tiles_f, columns, block_count, block_size):
    grad_blocks = field.reshape(field.shape[0], block_count, block_size)
    contrib = jnp.einsum('nbi,bjiq->nbjq', grad_blocks, tiles_f)
    summed = jnp.zeros_like(grad_blocks).at[:, columns].add(contrib)
    return summed.reshape(field.shape[0], block_count * block_size)

def reference(maps, cotangent, tiles, columns, filters):
    tiles_f = tiles.astype(jnp.float32)
    weights_f = filters.astype(jnp.float32)
    row_count = MAP_DEV * C

    def one_group(pair):
        map_group, cot_group = pair
        x_zero = map_group.astype(jnp.float32).reshape(row_count, NPIX)
        x_one = forward_apply(x_zero, tiles_f, columns, NBLK, BS).astype(jnp.bfloat16)
        x_two = (2.0 * forward_apply(x_one.astype(jnp.float32), tiles_f, columns, NBLK, BS) - x_zero).astype(jnp.bfloat16)
        terms = jnp.stack([map_group, x_one.reshape(MAP_DEV, C, NPIX), x_two.reshape(MAP_DEV, C, NPIX)]).astype(jnp.float32)
        output = jnp.einsum('kco,kmcp->mop', weights_f, terms).astype(jnp.bfloat16)
        cot_f = cot_group.astype(jnp.float32)
        grads = jnp.einsum('kco,mop->kmcp', weights_f, cot_f)
        grad_two = grads[2].astype(jnp.bfloat16).reshape(row_count, NPIX)
        adj_first = adjoint_apply(grad_two.astype(jnp.float32), tiles_f, columns, NBLK, BS)
        update = (grads[1].reshape(row_count, NPIX) + 2.0 * adj_first).astype(jnp.bfloat16)
        adj_second = adjoint_apply(update.astype(jnp.float32), tiles_f, columns, NBLK, BS)
        input_grad = (grads[0].reshape(row_count, NPIX) - grad_two.astype(jnp.float32) + adj_second).astype(jnp.bfloat16)
        partial_grad = jnp.einsum('kmcp,mop->kco', terms, cot_f)
        return (output, input_grad.reshape(MAP_DEV, C, NPIX), partial_grad)
    map_groups = maps.reshape(N_MAP, MAP_DEV, C, NPIX)
    cot_groups = cotangent.reshape(N_MAP, MAP_DEV, C, NPIX)
    outputs, input_grads, partials = lax.map(one_group, (map_groups, cot_groups))
    scale = 1.0 / math.sqrt(MAPS * NPIX)
    filter_grad = lax.optimization_barrier(jnp.sum(partials, axis=0)) * scale
    return (outputs.reshape(MAPS, C, NPIX), input_grads.reshape(MAPS, C, NPIX), filter_grad)
```

```python
import functools
import math

import jax
import jax.numpy as jnp
from jax import lax
from jax.experimental import pallas as pl
from jax.experimental.pallas import tpu as pltpu
from jax.sharding import PartitionSpec as P

REACH = 2
MESH = pl.DeviceIdType.MESH
F32 = jnp.float32
BF16 = jnp.bfloat16


def dot_nn(a, b):
    return lax.dot_general(a, b, (((1,), (0,)), ((), ())), preferred_element_type=F32)


def dot_nt(a, b):
    return lax.dot_general(a, b, (((1,), (1,)), ((), ())), preferred_element_type=F32)


def mixing(filters, copies):
    order, chan = filters.shape[0], filters.shape[1]
    zero = jnp.zeros((chan, chan), F32)
    adjoint, output = [], []
    for m in range(copies):
        adjoint.append([])
        output.append([])
        for k in list(range(order)) + [order - 1]:
            term = filters[k].astype(F32)
            for n in range(copies):
                adjoint[m].append(term if n == m else zero)
                output[m].append(term.T if n == m else zero)
    join = lambda rows: jnp.concatenate([jnp.concatenate(r, axis=1) for r in rows], axis=0).astype(BF16)
    return join(adjoint), join(output)


def kernel(
    patch_count,
    map_count,
    copies,
    scale,
    maps,
    cot,
    tiles_hbm,
    cols,
    filters,
    out,
    grad,
    filter_grad,
    tiles,
    x_zero,
    x_one,
    y_zero,
    y_one,
    acc_x,
    acc_y,
    to_left,
    to_right,
    from_left,
    from_right,
    sum_patch,
    sum_map,
    mix_out,
    mix_in,
    load_tile,
    load_x,
    load_y,
    halo_send,
    halo_recv,
    adj_send,
    adj_recv,
    patch_send,
    patch_recv,
    map_send,
    map_recv,
):
    nb, _, bs, _ = tiles.shape
    reach = REACH
    me, my_map = lax.axis_index("patch"), lax.axis_index("map")
    left = lax.rem(me + patch_count - 1, patch_count)
    right = lax.rem(me + 1, patch_count)
    total = patch_count * nb
    low = list(range(reach))
    high = list(range(nb - reach, nb))
    middle = list(range(reach, nb - reach))
    edges = [b for pair in zip(low, reversed(high)) for b in pair]
    order = edges + middle

    loads_y = [pltpu.make_async_copy(cot.at[:, pl.ds(b * bs, bs)], y_zero.at[b], load_y.at[b]) for b in range(nb)]
    loads_x = [pltpu.make_async_copy(maps.at[:, pl.ds(b * bs, bs)], x_zero.at[reach + b], load_x.at[b]) for b in range(nb)]
    loads_t = [pltpu.make_async_copy(tiles_hbm.at[b], tiles.at[b], load_tile.at[b]) for b in range(nb)]
    for b in order:
        loads_y[b].start()
        loads_t[b].start()
    for b in order:
        loads_x[b].start()

    barrier = pltpu.get_barrier_semaphore()
    for d in range(1, patch_count):
        pl.semaphore_signal(barrier, inc=1, device_id=(lax.rem(me + d, patch_count), my_map), device_id_type=MESH)
    for d in range(1, map_count):
        pl.semaphore_signal(barrier, inc=1, device_id=(me, lax.rem(my_map + d, map_count)), device_id_type=MESH)

    mix_in[...], mix_out[...] = mixing(filters, copies)
    near_left = [lax.rem(me * nb + b - cols[b, 1] + total, total) == 1 for b in range(nb)]
    near_right = [lax.rem(cols[b, 2] - me * nb - b + total, total) == 1 for b in range(nb)]

    pl.semaphore_wait(barrier, patch_count + map_count - 2)

    def remote(src, dst, send_sem, recv_sem, patch, map_index):
        copy = pltpu.make_async_remote_copy(
            src_ref=src,
            dst_ref=dst,
            send_sem=send_sem,
            recv_sem=recv_sem,
            device_id=(patch, map_index),
            device_id_type=MESH,
        )
        copy.start()
        return copy

    sent = []

    def send_halo(turn, source, field):
        copies_ = []
        for i in range(reach):
            copies_.append(
                remote(source(i), field.at[reach + nb + i], halo_send.at[turn, 0, i], halo_recv.at[turn, 0, i], left, my_map)
            )
            copies_.append(
                remote(
                    source(nb - reach + i), field.at[i], halo_send.at[turn, 1, i], halo_recv.at[turn, 1, i], right, my_map
                )
            )
        sent.extend(copies_)
        return copies_

    def pick(flag, yes, no):
        return jnp.where(flag, yes, no)

    def keep(flag, value):
        return jnp.where(flag, value, jnp.zeros_like(value))

    def left_part(w, b):
        return dot_nn(w[b], tiles[b, 1])

    def right_part(w, b):
        return dot_nn(w[b], tiles[b, 2])

    def send_adjoint(turn, w):
        p1 = {b: left_part(w, b) for b in low}
        p2 = {b: right_part(w, b) for b in high}
        last = nb - 1
        to_left[turn, 1] = (keep(near_left[0], p1[0]) + keep(~near_left[1], p1[1])).astype(BF16)
        to_left[turn, 0] = keep(~near_left[0], p1[0]).astype(BF16)
        to_right[turn, 0] = (keep(near_right[last], p2[last]) + keep(~near_right[last - 1], p2[last - 1])).astype(BF16)
        to_right[turn, 1] = keep(~near_right[last], p2[last]).astype(BF16)
        copies_ = [
            remote(to_left.at[turn], from_right.at[turn], adj_send.at[turn, 0], adj_recv.at[turn, 0], left, my_map),
            remote(to_right.at[turn], from_left.at[turn], adj_send.at[turn, 1], adj_recv.at[turn, 1], right, my_map),
        ]
        sent.extend(copies_)
        return copies_, p1, p2

    def local_adjoint(w, p1, p2):
        p1, p2 = dict(p1), dict(p2)
        for b in range(nb):
            if b not in p1:
                p1[b] = left_part(w, b)
            if b not in p2:
                p2[b] = right_part(w, b)
        for t in range(nb):
            value = dot_nn(w[t], tiles[t, 0])
            if t + 1 < nb:
                value = value + keep(near_left[t + 1], p1[t + 1])
            if t + 2 < nb:
                value = value + keep(~near_left[t + 2], p1[t + 2])
            if t >= 1:
                value = value + keep(near_right[t - 1], p2[t - 1])
            if t >= 2:
                value = value + keep(~near_right[t - 2], p2[t - 2])
            acc_y[t] = value

    def whole_adjoint(turn, t):
        value = acc_y[t]
        if t < reach:
            value = value + from_left[turn, t].astype(F32)
        if t >= nb - reach:
            value = value + from_right[turn, t - (nb - reach)].astype(F32)
        return value

    def own_term(field, b):
        return dot_nt(field[reach + b], tiles[b, 0])

    def left_term(field, b):
        return dot_nt(pick(near_left[b], field[reach + b - 1], field[reach + b - 2]), tiles[b, 1])

    def right_term(field, b):
        return dot_nt(pick(near_right[b], field[reach + b + 1], field[reach + b + 2]), tiles[b, 2])

    def inner_forward(field, b):
        value = own_term(field, b)
        if b >= reach:
            value = value + left_term(field, b)
        if b < nb - reach:
            value = value + right_term(field, b)
        return value

    def rest_forward(field, b):
        return left_term(field, b) if b < reach else right_term(field, b)

    halo = send_halo(0, lambda b: maps.at[:, pl.ds(b * bs, bs)], x_zero)
    for b in edges:
        loads_y[b].wait()
        loads_t[b].wait()
    adj, p1, p2 = send_adjoint(0, y_zero)
    for b in middle:
        loads_y[b].wait()
        loads_t[b].wait()
    for b in range(nb):
        loads_x[b].wait()
    for b in edges:
        acc_x[b] = inner_forward(x_zero, b)
    for copy in halo:
        copy.wait_recv()
    for b in edges:
        x_one[reach + b] = (acc_x[b] + rest_forward(x_zero, b)).astype(BF16)
    halo = send_halo(1, lambda b: x_one.at[reach + b], x_one)
    local_adjoint(y_zero, p1, p2)
    for copy in adj:
        copy.wait_recv()
    for b in range(nb):
        y_one[b] = whole_adjoint(0, b).astype(BF16)
    adj, p1, p2 = send_adjoint(1, y_one)
    for b in middle:
        x_one[reach + b] = inner_forward(x_zero, b).astype(BF16)

    chan = filters.shape[1]
    product = None
    for b in range(nb):
        rows = jnp.concatenate([x_zero[reach + b], x_one[reach + b]], axis=0)
        columns = jnp.concatenate([y_zero[b], y_one[b]], axis=0)
        term = dot_nt(rows, columns)
        product = term if product is None else product + term
    width = product.shape[1]
    half = copies * chan

    def fold(value):
        result = value[:chan]
        for m in range(1, copies):
            result = result + pltpu.roll(value[m * chan : (m + 1) * chan], width - m * chan, 1)
        return result

    with_zero, with_one = fold(product[:half]), fold(product[half:])
    lane = lax.broadcasted_iota(jnp.int32, (chan, width), 1)
    packed = jnp.where(
        lane < chan,
        with_zero,
        jnp.where(lane < 2 * chan, pltpu.roll(with_one, chan, 1), 2.0 * with_one - pltpu.roll(with_zero, half, 1)),
    )
    sum_patch[me] = packed
    over_patch = [
        remote(
            sum_patch.at[me],
            sum_patch.at[me],
            patch_send.at[d - 1],
            patch_recv.at[d - 1],
            lax.rem(me + d, patch_count),
            my_map,
        )
        for d in range(1, patch_count)
    ]
    sent.extend(over_patch)

    local_adjoint(y_one, p1, p2)
    for b in edges:
        acc_x[b] = inner_forward(x_one, b)

    def write_output(b, applied):
        first = x_zero[reach + b]
        x_two = (2.0 * applied - first.astype(F32)).astype(BF16)
        terms = jnp.concatenate([first, x_one[reach + b], x_two], axis=0)
        out[:, b * bs : (b + 1) * bs] = dot_nn(mix_out[:, : terms.shape[0]], terms).astype(BF16)

    def write_grad(b):
        first = y_zero[b]
        y_two = 2.0 * whole_adjoint(1, b) - first.astype(F32)
        coarse = y_two.astype(BF16)
        fine = (y_two - coarse.astype(F32)).astype(BF16)
        terms = jnp.concatenate([first, y_one[b], coarse, fine], axis=0)
        grad[:, b * bs : (b + 1) * bs] = dot_nn(mix_in[...], terms).astype(BF16)

    for copy in over_patch:
        copy.wait_recv()
    partial = sum_patch[0]
    for i in range(1, patch_count):
        partial = partial + sum_patch[i]
    sum_map[my_map] = partial
    over_map = [
        remote(
            sum_map.at[my_map],
            sum_map.at[my_map],
            map_send.at[d - 1],
            map_recv.at[d - 1],
            me,
            lax.rem(my_map + d, map_count),
        )
        for d in range(1, map_count)
    ]
    sent.extend(over_map)
    for b in middle:
        write_output(b, inner_forward(x_one, b))
        write_grad(b)
    for copy in halo:
        copy.wait_recv()
    for b in edges:
        write_output(b, acc_x[b] + rest_forward(x_one, b))
    for copy in adj:
        copy.wait_recv()
    for b in edges:
        write_grad(b)
    for copy in over_map:
        copy.wait_recv()
    whole = sum_map[0]
    for i in range(1, map_count):
        whole = whole + sum_map[i]
    whole = whole * scale
    for k in range(filters.shape[0]):
        shifted = pltpu.roll(whole, width - k * chan, 1) if k else whole
        filter_grad[k] = shifted[:, :chan]
    for copy in sent:
        copy.wait_send()


def per_device(patch_count, map_count, maps, cotangent, tiles, columns, filters):
    copies, chan, pix = maps.shape
    nb, slots, bs, _ = tiles.shape
    rows = copies * chan
    order = filters.shape[0]
    scale = 1.0 / math.sqrt(copies * map_count * pix * patch_count)
    any_space = pl.BlockSpec(memory_space=pl.ANY)
    vmem = pl.BlockSpec(memory_space=pltpu.VMEM)
    dma = pltpu.SemaphoreType.DMA
    field = pltpu.VMEM((nb + 2 * REACH, rows, bs), BF16)
    own = pltpu.VMEM((nb, rows, bs), BF16)
    wide = pltpu.VMEM((nb, rows, bs), F32)
    rim = pltpu.VMEM((2, REACH, rows, bs), BF16)
    packed = (chan, 2 * rows)
    out, grad, filter_grad = pl.pallas_call(
        functools.partial(kernel, patch_count, map_count, copies, scale),
        out_shape=(
            jax.ShapeDtypeStruct((rows, pix), BF16),
            jax.ShapeDtypeStruct((rows, pix), BF16),
            jax.ShapeDtypeStruct((order, chan, chan), F32),
        ),
        in_specs=[any_space, any_space, any_space, pl.BlockSpec(memory_space=pltpu.SMEM), vmem],
        out_specs=(vmem, vmem, vmem),
        scratch_shapes=[
            pltpu.VMEM((nb, slots, bs, bs), BF16),
            field,
            field,
            own,
            own,
            wide,
            wide,
            rim,
            rim,
            rim,
            rim,
            pltpu.VMEM((patch_count,) + packed, F32),
            pltpu.VMEM((map_count,) + packed, F32),
            pltpu.VMEM((rows, 4 * rows), BF16),
            pltpu.VMEM((rows, 4 * rows), BF16),
            dma((nb,)),
            dma((nb,)),
            dma((nb,)),
            dma((2, 2, REACH)),
            dma((2, 2, REACH)),
            dma((2, 2)),
            dma((2, 2)),
            dma((patch_count - 1,)),
            dma((patch_count - 1,)),
            dma((map_count - 1,)),
            dma((map_count - 1,)),
        ],
        compiler_params=pltpu.CompilerParams(
            collective_id=0, has_side_effects=True, vmem_limit_bytes=40 * 1024 * 1024
        ),
    )(maps.reshape(rows, pix), cotangent.reshape(rows, pix), tiles, columns, filters)
    return out.reshape(copies, chan, pix), grad.reshape(copies, chan, pix), filter_grad


def solution(mesh):
    field = P("map", None, "patch")
    return jax.shard_map(
        functools.partial(per_device, mesh.shape["patch"], mesh.shape["map"]),
        mesh=mesh,
        in_specs=(field, field, P("patch", None, None, None), P("patch", None), P()),
        out_specs=(field, field, P()),
        check_vma=False,
    )
```

```python
import functools
import math

import jax
import jax.numpy as jnp
from jax import lax
from jax.experimental import pallas as pl
from jax.experimental.pallas import tpu as pltpu
from jax.sharding import PartitionSpec as P

REACH = 2
MESH = pl.DeviceIdType.MESH
F32 = jnp.float32
BF16 = jnp.bfloat16


def dot_nn(a, b):
    return lax.dot_general(a, b, (((1,), (0,)), ((), ())), preferred_element_type=F32)


def dot_nt(a, b):
    return lax.dot_general(a, b, (((1,), (1,)), ((), ())), preferred_element_type=F32)


def mixing(filters, copies):
    order, chan = filters.shape[0], filters.shape[1]
    zero = jnp.zeros((chan, chan), F32)
    adjoint, output = [], []
    for m in range(copies):
        adjoint.append([])
        output.append([])
        for k in list(range(order)) + [order - 1]:
            term = filters[k].astype(F32)
            for n in range(copies):
                adjoint[m].append(term if n == m else zero)
                output[m].append(term.T if n == m else zero)
    join = lambda rows: jnp.concatenate([jnp.concatenate(r, axis=1) for r in rows], axis=0).astype(BF16)
    return join(adjoint), join(output)


def kernel(
    patch_count,
    map_count,
    copies,
    scale,
    maps,
    cot,
    tiles_hbm,
    cols_hbm,
    filters_hbm,
    out,
    grad,
    filter_grad,
    cols,
    filters,
    tiles,
    x_zero,
    x_one,
    y_zero,
    y_one,
    acc_x,
    acc_y,
    to_left,
    to_right,
    from_left,
    from_right,
    sum_patch,
    sum_map,
    mix_out,
    mix_in,
    load_cols,
    load_filters,
    load_tile,
    load_x,
    load_y,
    halo_send,
    halo_recv,
    adj_send,
    adj_recv,
    patch_send,
    patch_recv,
    map_send,
    map_recv,
):
    nb, _, bs, _ = tiles.shape
    reach = REACH
    me, my_map = lax.axis_index("patch"), lax.axis_index("map")
    left = lax.rem(me + patch_count - 1, patch_count)
    right = lax.rem(me + 1, patch_count)
    total = patch_count * nb
    low = list(range(reach))
    high = list(range(nb - reach, nb))
    middle = list(range(reach, nb - reach))
    edges = [b for pair in zip(low, reversed(high)) for b in pair]
    order = edges + middle

    loads_y = [pltpu.make_async_copy(cot.at[:, pl.ds(b * bs, bs)], y_zero.at[b], load_y.at[b]) for b in range(nb)]
    loads_x = [pltpu.make_async_copy(maps.at[:, pl.ds(b * bs, bs)], x_zero.at[reach + b], load_x.at[b]) for b in range(nb)]
    loads_t = [pltpu.make_async_copy(tiles_hbm.at[b], tiles.at[b], load_tile.at[b]) for b in range(nb)]
    for b in order:
        loads_y[b].start()
        loads_t[b].start()
    load_f = pltpu.make_async_copy(filters_hbm, filters, load_filters)
    load_f.start()
    load_c = pltpu.make_async_copy(cols_hbm, cols, load_cols)
    load_c.start()
    for b in order:
        loads_x[b].start()

    barrier = pltpu.get_barrier_semaphore()
    for d in range(1, patch_count):
        pl.semaphore_signal(barrier, inc=1, device_id=(lax.rem(me + d, patch_count), my_map), device_id_type=MESH)
    for d in range(1, map_count):
        pl.semaphore_signal(barrier, inc=1, device_id=(me, lax.rem(my_map + d, map_count)), device_id_type=MESH)

    load_f.wait()
    load_c.wait()
    mix_in[...], mix_out[...] = mixing(filters, copies)
    near_left = [lax.rem(me * nb + b - cols[1, b] + total, total) == 1 for b in range(nb)]
    near_right = [lax.rem(cols[2, b] - me * nb - b + total, total) == 1 for b in range(nb)]

    pl.semaphore_wait(barrier, patch_count + map_count - 2)

    def remote(src, dst, send_sem, recv_sem, patch, map_index):
        copy = pltpu.make_async_remote_copy(
            src_ref=src,
            dst_ref=dst,
            send_sem=send_sem,
            recv_sem=recv_sem,
            device_id=(patch, map_index),
            device_id_type=MESH,
        )
        copy.start()
        return copy

    sent = []

    def send_halo(turn, source, field):
        copies_ = []
        for i in range(reach):
            copies_.append(
                remote(source(i), field.at[reach + nb + i], halo_send.at[turn, 0, i], halo_recv.at[turn, 0, i], left, my_map)
            )
            copies_.append(
                remote(
                    source(nb - reach + i), field.at[i], halo_send.at[turn, 1, i], halo_recv.at[turn, 1, i], right, my_map
                )
            )
        sent.extend(copies_)
        return copies_

    def pick(flag, yes, no):
        return jnp.where(flag, yes, no)

    def keep(flag, value):
        return jnp.where(flag, value, jnp.zeros_like(value))

    def left_part(w, b):
        return dot_nn(w[b], tiles[b, 1])

    def right_part(w, b):
        return dot_nn(w[b], tiles[b, 2])

    def send_adjoint(turn, w):
        p1 = {b: left_part(w, b) for b in low}
        p2 = {b: right_part(w, b) for b in high}
        last = nb - 1
        to_left[turn, 1] = (keep(near_left[0], p1[0]) + keep(~near_left[1], p1[1])).astype(BF16)
        to_left[turn, 0] = keep(~near_left[0], p1[0]).astype(BF16)
        to_right[turn, 0] = (keep(near_right[last], p2[last]) + keep(~near_right[last - 1], p2[last - 1])).astype(BF16)
        to_right[turn, 1] = keep(~near_right[last], p2[last]).astype(BF16)
        copies_ = [
            remote(to_left.at[turn], from_right.at[turn], adj_send.at[turn, 0], adj_recv.at[turn, 0], left, my_map),
            remote(to_right.at[turn], from_left.at[turn], adj_send.at[turn, 1], adj_recv.at[turn, 1], right, my_map),
        ]
        sent.extend(copies_)
        return copies_, p1, p2

    def local_adjoint(w, p1, p2):
        p1, p2 = dict(p1), dict(p2)
        for b in range(nb):
            if b not in p1:
                p1[b] = left_part(w, b)
            if b not in p2:
                p2[b] = right_part(w, b)
        for t in range(nb):
            value = dot_nn(w[t], tiles[t, 0])
            if t + 1 < nb:
                value = value + keep(near_left[t + 1], p1[t + 1])
            if t + 2 < nb:
                value = value + keep(~near_left[t + 2], p1[t + 2])
            if t >= 1:
                value = value + keep(near_right[t - 1], p2[t - 1])
            if t >= 2:
                value = value + keep(~near_right[t - 2], p2[t - 2])
            acc_y[t] = value

    def whole_adjoint(turn, t):
        value = acc_y[t]
        if t < reach:
            value = value + from_left[turn, t].astype(F32)
        if t >= nb - reach:
            value = value + from_right[turn, t - (nb - reach)].astype(F32)
        return value

    def own_term(field, b):
        return dot_nt(field[reach + b], tiles[b, 0])

    def left_term(field, b):
        return dot_nt(pick(near_left[b], field[reach + b - 1], field[reach + b - 2]), tiles[b, 1])

    def right_term(field, b):
        return dot_nt(pick(near_right[b], field[reach + b + 1], field[reach + b + 2]), tiles[b, 2])

    def inner_forward(field, b):
        value = own_term(field, b)
        if b >= reach:
            value = value + left_term(field, b)
        if b < nb - reach:
            value = value + right_term(field, b)
        return value

    def rest_forward(field, b):
        return left_term(field, b) if b < reach else right_term(field, b)

    halo = send_halo(0, lambda b: maps.at[:, pl.ds(b * bs, bs)], x_zero)
    for b in edges:
        loads_y[b].wait()
        loads_t[b].wait()
    adj, p1, p2 = send_adjoint(0, y_zero)
    for b in middle:
        loads_y[b].wait()
        loads_t[b].wait()
    for b in range(nb):
        loads_x[b].wait()
    for b in edges:
        acc_x[b] = inner_forward(x_zero, b)
    for copy in halo:
        copy.wait_recv()
    for b in edges:
        x_one[reach + b] = (acc_x[b] + rest_forward(x_zero, b)).astype(BF16)
    halo = send_halo(1, lambda b: x_one.at[reach + b], x_one)
    local_adjoint(y_zero, p1, p2)
    for copy in adj:
        copy.wait_recv()
    for b in range(nb):
        y_one[b] = whole_adjoint(0, b).astype(BF16)
    adj, p1, p2 = send_adjoint(1, y_one)
    for b in middle:
        x_one[reach + b] = inner_forward(x_zero, b).astype(BF16)

    chan = filters.shape[1]
    product = None
    for b in range(nb):
        rows = jnp.concatenate([x_zero[reach + b], x_one[reach + b]], axis=0)
        columns = jnp.concatenate([y_zero[b], y_one[b]], axis=0)
        term = dot_nt(rows, columns)
        product = term if product is None else product + term
    width = product.shape[1]
    half = copies * chan

    def fold(value):
        result = value[:chan]
        for m in range(1, copies):
            result = result + pltpu.roll(value[m * chan : (m + 1) * chan], width - m * chan, 1)
        return result

    with_zero, with_one = fold(product[:half]), fold(product[half:])
    lane = lax.broadcasted_iota(jnp.int32, (chan, width), 1)
    packed = jnp.where(
        lane < chan,
        with_zero,
        jnp.where(lane < 2 * chan, pltpu.roll(with_one, chan, 1), 2.0 * with_one - pltpu.roll(with_zero, half, 1)),
    )
    sum_patch[me] = packed
    over_patch = [
        remote(
            sum_patch.at[me],
            sum_patch.at[me],
            patch_send.at[d - 1],
            patch_recv.at[d - 1],
            lax.rem(me + d, patch_count),
            my_map,
        )
        for d in range(1, patch_count)
    ]
    sent.extend(over_patch)

    local_adjoint(y_one, p1, p2)
    for b in edges:
        acc_x[b] = inner_forward(x_one, b)

    def write_output(b, applied):
        first = x_zero[reach + b]
        x_two = (2.0 * applied - first.astype(F32)).astype(BF16)
        terms = jnp.concatenate([first, x_one[reach + b], x_two], axis=0)
        out[:, b * bs : (b + 1) * bs] = dot_nn(mix_out[:, : terms.shape[0]], terms).astype(BF16)

    def write_grad(b):
        first = y_zero[b]
        y_two = 2.0 * whole_adjoint(1, b) - first.astype(F32)
        coarse = y_two.astype(BF16)
        fine = (y_two - coarse.astype(F32)).astype(BF16)
        terms = jnp.concatenate([first, y_one[b], coarse, fine], axis=0)
        grad[:, b * bs : (b + 1) * bs] = dot_nn(mix_in[...], terms).astype(BF16)

    for copy in over_patch:
        copy.wait_recv()
    partial = sum_patch[0]
    for i in range(1, patch_count):
        partial = partial + sum_patch[i]
    sum_map[my_map] = partial
    over_map = [
        remote(
            sum_map.at[my_map],
            sum_map.at[my_map],
            map_send.at[d - 1],
            map_recv.at[d - 1],
            me,
            lax.rem(my_map + d, map_count),
        )
        for d in range(1, map_count)
    ]
    sent.extend(over_map)
    for b in middle:
        write_output(b, inner_forward(x_one, b))
        write_grad(b)
    for copy in halo:
        copy.wait_recv()
    for b in edges:
        write_output(b, acc_x[b] + rest_forward(x_one, b))
    for copy in adj:
        copy.wait_recv()
    for b in edges:
        write_grad(b)
    for copy in over_map:
        copy.wait_recv()
    whole = sum_map[0]
    for i in range(1, map_count):
        whole = whole + sum_map[i]
    whole = whole * scale
    for k in range(filters.shape[0]):
        shifted = pltpu.roll(whole, width - k * chan, 1) if k else whole
        filter_grad[k] = shifted[:, :chan]
    for copy in sent:
        copy.wait_send()


def write(out, grad, filter_grad, out_hbm, grad_hbm, filter_grad_hbm, sems):
    copies = [
        pltpu.make_async_copy(out, out_hbm, sems.at[0]),
        pltpu.make_async_copy(grad, grad_hbm, sems.at[1]),
        pltpu.make_async_copy(filter_grad, filter_grad_hbm, sems.at[2]),
    ]
    for copy in copies:
        copy.start()
    for copy in copies:
        copy.wait()


def per_device(patch_count, map_count, maps, cotangent, tiles, columns, filters):
    copies, chan, pix = maps.shape
    nb, slots, bs, _ = tiles.shape
    rows = copies * chan
    order = filters.shape[0]
    scale = 1.0 / math.sqrt(copies * map_count * pix * patch_count)
    hbm = pl.BlockSpec(memory_space=pltpu.HBM)
    vmem = pl.BlockSpec(memory_space=pltpu.VMEM)
    dma = pltpu.SemaphoreType.DMA
    field = pltpu.VMEM((nb + 2 * REACH, rows, bs), BF16)
    own = pltpu.VMEM((nb, rows, bs), BF16)
    wide = pltpu.VMEM((nb, rows, bs), F32)
    rim = pltpu.VMEM((2, REACH, rows, bs), BF16)
    packed = (chan, 2 * rows)
    pin = lambda x: pltpu.with_memory_space_constraint(x, pltpu.HBM)
    results = (
        jax.ShapeDtypeStruct((rows, pix), BF16),
        jax.ShapeDtypeStruct((rows, pix), BF16),
        jax.ShapeDtypeStruct((order, chan, chan), F32),
    )
    held = pl.pallas_call(
        functools.partial(kernel, patch_count, map_count, copies, scale),
        out_shape=results,
        in_specs=[hbm, hbm, hbm, hbm, hbm],
        out_specs=(vmem, vmem, vmem),
        scratch_shapes=[
            pltpu.SMEM((slots, nb), jnp.int32),
            pltpu.VMEM((order, chan, chan), BF16),
            pltpu.VMEM((nb, slots, bs, bs), BF16),
            field,
            field,
            own,
            own,
            wide,
            wide,
            rim,
            rim,
            rim,
            rim,
            pltpu.VMEM((patch_count,) + packed, F32),
            pltpu.VMEM((map_count,) + packed, F32),
            pltpu.VMEM((rows, 4 * rows), BF16),
            pltpu.VMEM((rows, 4 * rows), BF16),
            dma,
            dma,
            dma((nb,)),
            dma((nb,)),
            dma((nb,)),
            dma((2, 2, REACH)),
            dma((2, 2, REACH)),
            dma((2, 2)),
            dma((2, 2)),
            dma((patch_count - 1,)),
            dma((patch_count - 1,)),
            dma((map_count - 1,)),
            dma((map_count - 1,)),
        ],
        compiler_params=pltpu.CompilerParams(
            collective_id=0, has_side_effects=True, vmem_limit_bytes=40 * 1024 * 1024
        ),
    )(
        pin(maps.reshape(rows, pix)), pin(cotangent.reshape(rows, pix)), pin(tiles), pin(columns.T), pin(filters)
    )
    out, grad, filter_grad = pl.pallas_call(
        write,
        out_shape=results,
        in_specs=[vmem] * 3,
        out_specs=(hbm,) * 3,
        scratch_shapes=[dma((3,))],
    )(*held)
    return out.reshape(copies, chan, pix), grad.reshape(copies, chan, pix), filter_grad


def solution(mesh):
    field = P("map", None, "patch")
    return jax.shard_map(
        functools.partial(per_device, mesh.shape["patch"], mesh.shape["map"]),
        mesh=mesh,
        in_specs=(field, field, P("patch", None, None, None), P("patch", None), P()),
        out_specs=(field, field, P()),
        check_vma=False,
    )
```

```python
import functools
import math

import jax
import jax.numpy as jnp
from jax import lax
from jax.experimental import pallas as pl
from jax.experimental.pallas import tpu as pltpu
from jax.sharding import PartitionSpec as P

REACH = 2
MESH = pl.DeviceIdType.MESH
F32 = jnp.float32
BF16 = jnp.bfloat16


def dot_nn(a, b):
    return lax.dot_general(a, b, (((1,), (0,)), ((), ())), preferred_element_type=F32)


def dot_nt(a, b):
    return lax.dot_general(a, b, (((1,), (1,)), ((), ())), preferred_element_type=F32)


def mixing(filters, copies):
    order, chan = filters.shape[0], filters.shape[1]
    zero = jnp.zeros((chan, chan), F32)
    adjoint, output = [], []
    for m in range(copies):
        adjoint.append([])
        output.append([])
        for k in list(range(order)) + [order - 1]:
            term = filters[k].astype(F32)
            for n in range(copies):
                adjoint[m].append(term if n == m else zero)
                output[m].append(term.T if n == m else zero)
    join = lambda rows: jnp.concatenate([jnp.concatenate(r, axis=1) for r in rows], axis=0).astype(BF16)
    return join(adjoint), join(output)


def kernel(
    patch_count,
    map_count,
    copies,
    scale,
    maps,
    cot,
    tiles_hbm,
    cols_hbm,
    filters_hbm,
    out,
    grad,
    filter_grad,
    cols,
    filters,
    tiles,
    turned_tiles,
    x_zero,
    x_one,
    y_zero,
    y_one,
    acc_x,
    acc_y,
    to_left,
    to_right,
    from_left,
    from_right,
    sum_patch,
    sum_map,
    mix_out,
    mix_in,
    load_cols,
    load_filters,
    load_tile,
    load_x,
    load_y,
    halo_send,
    halo_recv,
    adj_send,
    adj_recv,
    patch_send,
    patch_recv,
    map_send,
    map_recv,
):
    nb, _, bs, _ = tiles.shape
    reach = REACH
    me, my_map = lax.axis_index("patch"), lax.axis_index("map")
    left = lax.rem(me + patch_count - 1, patch_count)
    right = lax.rem(me + 1, patch_count)
    total = patch_count * nb
    low = list(range(reach))
    high = list(range(nb - reach, nb))
    middle = list(range(reach, nb - reach))
    edges = [b for pair in zip(low, reversed(high)) for b in pair]
    order = edges + middle

    loads_y = [pltpu.make_async_copy(cot.at[:, pl.ds(b * bs, bs)], y_zero.at[b], load_y.at[b]) for b in range(nb)]
    loads_x = [pltpu.make_async_copy(maps.at[:, pl.ds(b * bs, bs)], x_zero.at[reach + b], load_x.at[b]) for b in range(nb)]
    loads_t = [pltpu.make_async_copy(tiles_hbm.at[b], tiles.at[b], load_tile.at[b]) for b in range(nb)]
    for b in order:
        loads_y[b].start()
        loads_t[b].start()
    load_f = pltpu.make_async_copy(filters_hbm, filters, load_filters)
    load_f.start()
    load_c = pltpu.make_async_copy(cols_hbm, cols, load_cols)
    load_c.start()
    for b in order:
        loads_x[b].start()

    barrier = pltpu.get_barrier_semaphore()
    for d in range(1, patch_count):
        pl.semaphore_signal(barrier, inc=1, device_id=(lax.rem(me + d, patch_count), my_map), device_id_type=MESH)
    for d in range(1, map_count):
        pl.semaphore_signal(barrier, inc=1, device_id=(me, lax.rem(my_map + d, map_count)), device_id_type=MESH)

    load_f.wait()
    load_c.wait()
    mix_in[...], mix_out[...] = mixing(filters, copies)
    near_left = [lax.rem(me * nb + b - cols[1, b] + total, total) == 1 for b in range(nb)]
    near_right = [lax.rem(cols[2, b] - me * nb - b + total, total) == 1 for b in range(nb)]

    pl.semaphore_wait(barrier, patch_count + map_count - 2)

    def remote(src, dst, send_sem, recv_sem, patch, map_index):
        copy = pltpu.make_async_remote_copy(
            src_ref=src,
            dst_ref=dst,
            send_sem=send_sem,
            recv_sem=recv_sem,
            device_id=(patch, map_index),
            device_id_type=MESH,
        )
        copy.start()
        return copy

    sent = []

    def send_halo(turn, source, field):
        copies_ = []
        for i in range(reach):
            copies_.append(
                remote(source(i), field.at[reach + nb + i], halo_send.at[turn, 0, i], halo_recv.at[turn, 0, i], left, my_map)
            )
            copies_.append(
                remote(
                    source(nb - reach + i), field.at[i], halo_send.at[turn, 1, i], halo_recv.at[turn, 1, i], right, my_map
                )
            )
        sent.extend(copies_)
        return copies_

    def pick(flag, yes, no):
        return jnp.where(flag, yes, no)

    def keep(flag, value):
        return jnp.where(flag, value, jnp.zeros_like(value))

    def left_part(w, b):
        return dot_nn(w[b], tiles[b, 1])

    def right_part(w, b):
        return dot_nn(w[b], tiles[b, 2])

    def send_adjoint(turn, w):
        p1 = {b: left_part(w, b) for b in low}
        p2 = {b: right_part(w, b) for b in high}
        last = nb - 1
        to_left[turn, 1] = (keep(near_left[0], p1[0]) + keep(~near_left[1], p1[1])).astype(BF16)
        to_left[turn, 0] = keep(~near_left[0], p1[0]).astype(BF16)
        to_right[turn, 0] = (keep(near_right[last], p2[last]) + keep(~near_right[last - 1], p2[last - 1])).astype(BF16)
        to_right[turn, 1] = keep(~near_right[last], p2[last]).astype(BF16)
        copies_ = [
            remote(to_left.at[turn], from_right.at[turn], adj_send.at[turn, 0], adj_recv.at[turn, 0], left, my_map),
            remote(to_right.at[turn], from_left.at[turn], adj_send.at[turn, 1], adj_recv.at[turn, 1], right, my_map),
        ]
        sent.extend(copies_)
        return copies_, p1, p2

    def local_adjoint(w, p1, p2):
        p1, p2 = dict(p1), dict(p2)
        for b in range(nb):
            if b not in p1:
                p1[b] = left_part(w, b)
            if b not in p2:
                p2[b] = right_part(w, b)
        for t in range(nb):
            value = dot_nn(w[t], tiles[t, 0])
            if t + 1 < nb:
                value = value + keep(near_left[t + 1], p1[t + 1])
            if t + 2 < nb:
                value = value + keep(~near_left[t + 2], p1[t + 2])
            if t >= 1:
                value = value + keep(near_right[t - 1], p2[t - 1])
            if t >= 2:
                value = value + keep(~near_right[t - 2], p2[t - 2])
            acc_y[t] = value

    def whole_adjoint(turn, t):
        value = acc_y[t]
        if t < reach:
            value = value + from_left[turn, t].astype(F32)
        if t >= nb - reach:
            value = value + from_right[turn, t - (nb - reach)].astype(F32)
        return value

    def turned(field, b, slot):
        if field is x_zero:
            turned_tiles[b, slot] = tiles[b, slot].T
        return turned_tiles[b, slot]

    def own_term(field, b):
        return dot_nn(field[reach + b], turned(field, b, 0))

    def left_term(field, b):
        return dot_nn(pick(near_left[b], field[reach + b - 1], field[reach + b - 2]), turned(field, b, 1))

    def right_term(field, b):
        return dot_nn(pick(near_right[b], field[reach + b + 1], field[reach + b + 2]), turned(field, b, 2))

    def inner_forward(field, b):
        value = own_term(field, b)
        if b >= reach:
            value = value + left_term(field, b)
        if b < nb - reach:
            value = value + right_term(field, b)
        return value

    def rest_forward(field, b):
        return left_term(field, b) if b < reach else right_term(field, b)

    halo = send_halo(0, lambda b: maps.at[:, pl.ds(b * bs, bs)], x_zero)
    for b in edges:
        loads_y[b].wait()
        loads_t[b].wait()
    adj, p1, p2 = send_adjoint(0, y_zero)
    for b in middle:
        loads_y[b].wait()
        loads_t[b].wait()
    for b in range(nb):
        loads_x[b].wait()
    for b in edges:
        acc_x[b] = inner_forward(x_zero, b)
    for copy in halo:
        copy.wait_recv()
    for b in edges:
        x_one[reach + b] = (acc_x[b] + rest_forward(x_zero, b)).astype(BF16)
    halo = send_halo(1, lambda b: x_one.at[reach + b], x_one)
    local_adjoint(y_zero, p1, p2)
    for copy in adj:
        copy.wait_recv()
    for b in range(nb):
        y_one[b] = whole_adjoint(0, b).astype(BF16)
    adj, p1, p2 = send_adjoint(1, y_one)
    for b in middle:
        x_one[reach + b] = inner_forward(x_zero, b).astype(BF16)

    chan = filters.shape[1]
    product = None
    for b in range(nb):
        rows = jnp.concatenate([x_zero[reach + b], x_one[reach + b]], axis=0)
        columns = jnp.concatenate([y_zero[b], y_one[b]], axis=0)
        term = dot_nt(rows, columns)
        product = term if product is None else product + term
    width = product.shape[1]
    half = copies * chan

    def fold(value):
        result = value[:chan]
        for m in range(1, copies):
            result = result + pltpu.roll(value[m * chan : (m + 1) * chan], width - m * chan, 1)
        return result

    with_zero, with_one = fold(product[:half]), fold(product[half:])
    lane = lax.broadcasted_iota(jnp.int32, (chan, width), 1)
    packed = jnp.where(
        lane < chan,
        with_zero,
        jnp.where(lane < 2 * chan, pltpu.roll(with_one, chan, 1), 2.0 * with_one - pltpu.roll(with_zero, half, 1)),
    )
    sum_patch[me] = packed
    over_patch = [
        remote(
            sum_patch.at[me],
            sum_patch.at[me],
            patch_send.at[d - 1],
            patch_recv.at[d - 1],
            lax.rem(me + d, patch_count),
            my_map,
        )
        for d in range(1, patch_count)
    ]
    sent.extend(over_patch)

    local_adjoint(y_one, p1, p2)
    for b in edges:
        acc_x[b] = inner_forward(x_one, b)

    def write_output(b, applied):
        first = x_zero[reach + b]
        x_two = (2.0 * applied - first.astype(F32)).astype(BF16)
        terms = jnp.concatenate([first, x_one[reach + b], x_two], axis=0)
        out[:, b * bs : (b + 1) * bs] = dot_nn(mix_out[:, : terms.shape[0]], terms).astype(BF16)

    def write_grad(b):
        first = y_zero[b]
        y_two = 2.0 * whole_adjoint(1, b) - first.astype(F32)
        coarse = y_two.astype(BF16)
        fine = (y_two - coarse.astype(F32)).astype(BF16)
        terms = jnp.concatenate([first, y_one[b], coarse, fine], axis=0)
        grad[:, b * bs : (b + 1) * bs] = dot_nn(mix_in[...], terms).astype(BF16)

    for copy in over_patch:
        copy.wait_recv()
    partial = sum_patch[0]
    for i in range(1, patch_count):
        partial = partial + sum_patch[i]
    sum_map[my_map] = partial
    over_map = [
        remote(
            sum_map.at[my_map],
            sum_map.at[my_map],
            map_send.at[d - 1],
            map_recv.at[d - 1],
            me,
            lax.rem(my_map + d, map_count),
        )
        for d in range(1, map_count)
    ]
    sent.extend(over_map)
    for b in middle:
        write_output(b, inner_forward(x_one, b))
        write_grad(b)
    for copy in halo:
        copy.wait_recv()
    for b in edges:
        write_output(b, acc_x[b] + rest_forward(x_one, b))
    for copy in adj:
        copy.wait_recv()
    for b in edges:
        write_grad(b)
    for copy in over_map:
        copy.wait_recv()
    whole = sum_map[0]
    for i in range(1, map_count):
        whole = whole + sum_map[i]
    whole = whole * scale
    for k in range(filters.shape[0]):
        shifted = pltpu.roll(whole, width - k * chan, 1) if k else whole
        filter_grad[k] = shifted[:, :chan]
    for copy in sent:
        copy.wait_send()


def write(out, grad, filter_grad, out_hbm, grad_hbm, filter_grad_hbm, sems):
    copies = [
        pltpu.make_async_copy(out, out_hbm, sems.at[0]),
        pltpu.make_async_copy(grad, grad_hbm, sems.at[1]),
        pltpu.make_async_copy(filter_grad, filter_grad_hbm, sems.at[2]),
    ]
    for copy in copies:
        copy.start()
    for copy in copies:
        copy.wait()


def per_device(patch_count, map_count, maps, cotangent, tiles, columns, filters):
    copies, chan, pix = maps.shape
    nb, slots, bs, _ = tiles.shape
    rows = copies * chan
    order = filters.shape[0]
    scale = 1.0 / math.sqrt(copies * map_count * pix * patch_count)
    hbm = pl.BlockSpec(memory_space=pltpu.HBM)
    vmem = pl.BlockSpec(memory_space=pltpu.VMEM)
    dma = pltpu.SemaphoreType.DMA
    field = pltpu.VMEM((nb + 2 * REACH, rows, bs), BF16)
    own = pltpu.VMEM((nb, rows, bs), BF16)
    wide = pltpu.VMEM((nb, rows, bs), F32)
    rim = pltpu.VMEM((2, REACH, rows, bs), BF16)
    packed = (chan, 2 * rows)
    pin = lambda x: pltpu.with_memory_space_constraint(x, pltpu.HBM)
    results = (
        jax.ShapeDtypeStruct((rows, pix), BF16),
        jax.ShapeDtypeStruct((rows, pix), BF16),
        jax.ShapeDtypeStruct((order, chan, chan), F32),
    )
    held = pl.pallas_call(
        functools.partial(kernel, patch_count, map_count, copies, scale),
        out_shape=results,
        in_specs=[hbm, hbm, hbm, hbm, hbm],
        out_specs=(vmem, vmem, vmem),
        scratch_shapes=[
            pltpu.SMEM((slots, nb), jnp.int32),
            pltpu.VMEM((order, chan, chan), BF16),
            pltpu.VMEM((nb, slots, bs, bs), BF16),
            pltpu.VMEM((nb, slots, bs, bs), BF16),
            field,
            field,
            own,
            own,
            wide,
            wide,
            rim,
            rim,
            rim,
            rim,
            pltpu.VMEM((patch_count,) + packed, F32),
            pltpu.VMEM((map_count,) + packed, F32),
            pltpu.VMEM((rows, 4 * rows), BF16),
            pltpu.VMEM((rows, 4 * rows), BF16),
            dma,
            dma,
            dma((nb,)),
            dma((nb,)),
            dma((nb,)),
            dma((2, 2, REACH)),
            dma((2, 2, REACH)),
            dma((2, 2)),
            dma((2, 2)),
            dma((patch_count - 1,)),
            dma((patch_count - 1,)),
            dma((map_count - 1,)),
            dma((map_count - 1,)),
        ],
        compiler_params=pltpu.CompilerParams(
            collective_id=0, has_side_effects=True, vmem_limit_bytes=40 * 1024 * 1024
        ),
    )(
        pin(maps.reshape(rows, pix)), pin(cotangent.reshape(rows, pix)), pin(tiles), pin(columns.T), pin(filters)
    )
    out, grad, filter_grad = pl.pallas_call(
        write,
        out_shape=results,
        in_specs=[vmem] * 3,
        out_specs=(hbm,) * 3,
        scratch_shapes=[dma((3,))],
        compiler_params=pltpu.CompilerParams(vmem_limit_bytes=4 * 1024 * 1024),
    )(*held)
    return out.reshape(copies, chan, pix), grad.reshape(copies, chan, pix), filter_grad


def solution(mesh):
    field = P("map", None, "patch")
    return jax.shard_map(
        functools.partial(per_device, mesh.shape["patch"], mesh.shape["map"]),
        mesh=mesh,
        in_specs=(field, field, P("patch", None, None, None), P("patch", None), P()),
        out_specs=(field, field, P()),
        check_vma=False,
    )
```

```python
import functools
import math

import jax
import jax.numpy as jnp
from jax import lax
from jax.experimental import pallas as pl
from jax.experimental.pallas import tpu as pltpu
from jax.sharding import PartitionSpec as P

REACH = 2
MESH = pl.DeviceIdType.MESH
F32 = jnp.float32
BF16 = jnp.bfloat16


def dot_nn(a, b):
    return lax.dot_general(a, b, (((1,), (0,)), ((), ())), preferred_element_type=F32)


def dot_nt(a, b):
    return lax.dot_general(a, b, (((1,), (1,)), ((), ())), preferred_element_type=F32)


def mixing(filters, copies):
    order, chan = filters.shape[0], filters.shape[1]
    zero = jnp.zeros((chan, chan), F32)
    adjoint, output = [], []
    for m in range(copies):
        adjoint.append([])
        output.append([])
        for k in list(range(order)) + [order - 1]:
            term = filters[k].astype(F32)
            for n in range(copies):
                adjoint[m].append(term if n == m else zero)
                output[m].append(term.T if n == m else zero)
    join = lambda rows: jnp.concatenate([jnp.concatenate(r, axis=1) for r in rows], axis=0).astype(BF16)
    return join(adjoint), join(output)


def kernel(
    patch_count,
    map_count,
    copies,
    scale,
    maps,
    cot,
    tiles_hbm,
    cols_hbm,
    filters_hbm,
    out,
    grad,
    filter_grad,
    cols,
    filters,
    tiles,
    turned_tiles,
    x_zero,
    x_one,
    y_zero,
    y_one,
    acc_x,
    acc_y,
    to_left,
    to_right,
    from_left,
    from_right,
    terms_ref,
    sum_patch,
    sum_map,
    whole_ref,
    mix_out,
    mix_in,
    load_cols,
    load_filters,
    load_tile,
    load_x,
    load_y,
    halo_send,
    halo_recv,
    adj_send,
    adj_recv,
    patch_send,
    patch_recv,
    map_send,
    map_recv,
    gather_send,
    gather_recv,
):
    nb, _, bs, _ = tiles.shape
    reach = REACH
    me, my_map = lax.axis_index("patch"), lax.axis_index("map")
    left = lax.rem(me + patch_count - 1, patch_count)
    right = lax.rem(me + 1, patch_count)
    total = patch_count * nb
    low = list(range(reach))
    high = list(range(nb - reach, nb))
    middle = list(range(reach, nb - reach))
    edges = [b for pair in zip(low, reversed(high)) for b in pair]
    order = edges + middle

    loads_y = [pltpu.make_async_copy(cot.at[:, pl.ds(b * bs, bs)], y_zero.at[b], load_y.at[b]) for b in range(nb)]
    loads_x = [pltpu.make_async_copy(maps.at[:, pl.ds(b * bs, bs)], x_zero.at[reach + b], load_x.at[b]) for b in range(nb)]
    loads_t = [pltpu.make_async_copy(tiles_hbm.at[b], tiles.at[b], load_tile.at[b]) for b in range(nb)]
    for b in order:
        loads_y[b].start()
        loads_t[b].start()
    load_f = pltpu.make_async_copy(filters_hbm, filters, load_filters)
    load_f.start()
    load_c = pltpu.make_async_copy(cols_hbm, cols, load_cols)
    load_c.start()
    for b in order:
        loads_x[b].start()

    barrier = pltpu.get_barrier_semaphore()
    for d in range(1, patch_count):
        pl.semaphore_signal(barrier, inc=1, device_id=(lax.rem(me + d, patch_count), my_map), device_id_type=MESH)
    for d in range(1, map_count):
        pl.semaphore_signal(barrier, inc=1, device_id=(me, lax.rem(my_map + d, map_count)), device_id_type=MESH)

    load_f.wait()
    load_c.wait()
    mix_in[...], mix_out[...] = mixing(filters, copies)
    near_left = [lax.rem(me * nb + b - cols[1, b] + total, total) == 1 for b in range(nb)]
    near_right = [lax.rem(cols[2, b] - me * nb - b + total, total) == 1 for b in range(nb)]

    pl.semaphore_wait(barrier, patch_count + map_count - 2)

    def remote(src, dst, send_sem, recv_sem, patch, map_index):
        copy = pltpu.make_async_remote_copy(
            src_ref=src,
            dst_ref=dst,
            send_sem=send_sem,
            recv_sem=recv_sem,
            device_id=(patch, map_index),
            device_id_type=MESH,
        )
        copy.start()
        return copy

    sent = []

    def send_halo(turn, source, field):
        copies_ = []
        for i in range(reach):
            copies_.append(
                remote(source(i), field.at[reach + nb + i], halo_send.at[turn, 0, i], halo_recv.at[turn, 0, i], left, my_map)
            )
            copies_.append(
                remote(
                    source(nb - reach + i), field.at[i], halo_send.at[turn, 1, i], halo_recv.at[turn, 1, i], right, my_map
                )
            )
        sent.extend(copies_)
        return copies_

    def pick(flag, yes, no):
        return jnp.where(flag, yes, no)

    def keep(flag, value):
        return jnp.where(flag, value, jnp.zeros_like(value))

    def left_part(w, b):
        return dot_nn(w[b], tiles[b, 1])

    def right_part(w, b):
        return dot_nn(w[b], tiles[b, 2])

    def send_adjoint(turn, w):
        p1 = {b: left_part(w, b) for b in low}
        p2 = {b: right_part(w, b) for b in high}
        last = nb - 1
        to_left[turn, 1] = (keep(near_left[0], p1[0]) + keep(~near_left[1], p1[1])).astype(BF16)
        to_left[turn, 0] = keep(~near_left[0], p1[0]).astype(BF16)
        to_right[turn, 0] = (keep(near_right[last], p2[last]) + keep(~near_right[last - 1], p2[last - 1])).astype(BF16)
        to_right[turn, 1] = keep(~near_right[last], p2[last]).astype(BF16)
        copies_ = [
            remote(to_left.at[turn], from_right.at[turn], adj_send.at[turn, 0], adj_recv.at[turn, 0], left, my_map),
            remote(to_right.at[turn], from_left.at[turn], adj_send.at[turn, 1], adj_recv.at[turn, 1], right, my_map),
        ]
        sent.extend(copies_)
        return copies_, p1, p2

    def local_adjoint(w, p1, p2):
        p1, p2 = dict(p1), dict(p2)
        for b in range(nb):
            if b not in p1:
                p1[b] = left_part(w, b)
            if b not in p2:
                p2[b] = right_part(w, b)
        for t in range(nb):
            value = dot_nn(w[t], tiles[t, 0])
            if t + 1 < nb:
                value = value + keep(near_left[t + 1], p1[t + 1])
            if t + 2 < nb:
                value = value + keep(~near_left[t + 2], p1[t + 2])
            if t >= 1:
                value = value + keep(near_right[t - 1], p2[t - 1])
            if t >= 2:
                value = value + keep(~near_right[t - 2], p2[t - 2])
            acc_y[t] = value

    def whole_adjoint(turn, t):
        value = acc_y[t]
        if t < reach:
            value = value + from_left[turn, t].astype(F32)
        if t >= nb - reach:
            value = value + from_right[turn, t - (nb - reach)].astype(F32)
        return value

    def turned(field, b, slot):
        if field is x_zero:
            turned_tiles[b, slot] = tiles[b, slot].T
        return turned_tiles[b, slot]

    def own_term(field, b):
        return dot_nn(field[reach + b], turned(field, b, 0))

    def left_term(field, b):
        return dot_nn(pick(near_left[b], field[reach + b - 1], field[reach + b - 2]), turned(field, b, 1))

    def right_term(field, b):
        return dot_nn(pick(near_right[b], field[reach + b + 1], field[reach + b + 2]), turned(field, b, 2))

    def inner_forward(field, b):
        value = own_term(field, b)
        if b >= reach:
            value = value + left_term(field, b)
        if b < nb - reach:
            value = value + right_term(field, b)
        return value

    def rest_forward(field, b):
        return left_term(field, b) if b < reach else right_term(field, b)

    halo = send_halo(0, lambda b: maps.at[:, pl.ds(b * bs, bs)], x_zero)
    for b in edges:
        loads_y[b].wait()
        loads_t[b].wait()
    adj, p1, p2 = send_adjoint(0, y_zero)
    for b in range(nb):
        loads_x[b].wait()
    for b in edges:
        acc_x[b] = inner_forward(x_zero, b)
    for b in middle:
        loads_y[b].wait()
        loads_t[b].wait()
    local_adjoint(y_zero, p1, p2)
    for copy in halo:
        copy.wait_recv()
    for b in edges:
        x_one[reach + b] = (acc_x[b] + rest_forward(x_zero, b)).astype(BF16)
    halo = send_halo(1, lambda b: x_one.at[reach + b], x_one)
    for b in middle:
        x_one[reach + b] = inner_forward(x_zero, b).astype(BF16)
    for copy in adj:
        copy.wait_recv()
    for b in range(nb):
        y_one[b] = whole_adjoint(0, b).astype(BF16)

    chan = filters.shape[1]
    product = None
    for b in range(nb):
        rows = jnp.concatenate([x_zero[reach + b], x_one[reach + b]], axis=0)
        columns = jnp.concatenate([y_zero[b], y_one[b]], axis=0)
        term = dot_nt(rows, columns)
        product = term if product is None else product + term
    width = product.shape[1]
    half = copies * chan

    def fold(value):
        result = value[:chan]
        for m in range(1, copies):
            result = result + pltpu.roll(value[m * chan : (m + 1) * chan], width - m * chan, 1)
        return result

    with_zero, with_one = fold(product[:half]), fold(product[half:])
    lane = lax.broadcasted_iota(jnp.int32, (chan, width), 1)
    terms_ref[...] = jnp.where(
        lane < chan,
        with_zero,
        jnp.where(lane < 2 * chan, pltpu.roll(with_one, chan, 1), 2.0 * with_one - pltpu.roll(with_zero, half, 1)),
    )
    lines = sum_patch.shape[1]
    pieces = chan // lines

    def piece_of(device):
        return pl.ds(pl.multiple_of(lax.rem(device, pieces) * lines, lines), lines)

    sum_patch[me] = terms_ref[piece_of(me), :]
    over_patch = []
    for d in range(1, patch_count):
        peer = lax.rem(me + d, patch_count)
        over_patch.append(
            remote(
                terms_ref.at[piece_of(peer), :],
                sum_patch.at[me],
                patch_send.at[d - 1],
                patch_recv.at[d - 1],
                peer,
                my_map,
            )
        )
    sent.extend(over_patch)

    adj, p1, p2 = send_adjoint(1, y_one)
    for b in edges:
        acc_x[b] = inner_forward(x_one, b)

    def write_output(b, applied):
        first = x_zero[reach + b]
        x_two = (2.0 * applied - first.astype(F32)).astype(BF16)
        terms = jnp.concatenate([first, x_one[reach + b], x_two], axis=0)
        out[:, b * bs : (b + 1) * bs] = dot_nn(mix_out[:, : terms.shape[0]], terms).astype(BF16)

    def write_grad(b):
        first = y_zero[b]
        y_two = 2.0 * whole_adjoint(1, b) - first.astype(F32)
        coarse = y_two.astype(BF16)
        fine = (y_two - coarse.astype(F32)).astype(BF16)
        terms = jnp.concatenate([first, y_one[b], coarse, fine], axis=0)
        grad[:, b * bs : (b + 1) * bs] = dot_nn(mix_in[...], terms).astype(BF16)

    for copy in over_patch:
        copy.wait_recv()
    partial = sum_patch[0]
    for i in range(1, patch_count):
        partial = partial + sum_patch[i]
    sum_map[my_map] = partial
    over_map = [
        remote(
            sum_map.at[my_map],
            sum_map.at[my_map],
            map_send.at[d - 1],
            map_recv.at[d - 1],
            me,
            lax.rem(my_map + d, map_count),
        )
        for d in range(1, map_count)
    ]
    sent.extend(over_map)
    local_adjoint(y_one, p1, p2)
    for b in middle:
        write_output(b, inner_forward(x_one, b))
        write_grad(b)
    for copy in halo:
        copy.wait_recv()
    for b in edges:
        write_output(b, acc_x[b] + rest_forward(x_one, b))
    for copy in over_map:
        copy.wait_recv()
    whole = sum_map[0]
    for i in range(1, map_count):
        whole = whole + sum_map[i]
    whole_ref[piece_of(me), :] = whole * scale
    base = me - lax.rem(me, pieces)
    gathered = []
    for d in range(1, pieces):
        gathered.append(
            remote(
                whole_ref.at[piece_of(me), :],
                whole_ref.at[piece_of(me), :],
                gather_send.at[d - 1],
                gather_recv.at[d - 1],
                base + lax.rem(me + d, pieces),
                my_map,
            )
        )
    sent.extend(gathered)
    for copy in adj:
        copy.wait_recv()
    for b in edges:
        write_grad(b)
    for copy in gathered:
        copy.wait_recv()
    whole = whole_ref[...]
    for k in range(filters.shape[0]):
        shifted = pltpu.roll(whole, width - k * chan, 1) if k else whole
        filter_grad[k] = shifted[:, :chan]
    for copy in sent:
        copy.wait_send()


def write(out, grad, filter_grad, out_hbm, grad_hbm, filter_grad_hbm, sems):
    copies = [
        pltpu.make_async_copy(out, out_hbm, sems.at[0]),
        pltpu.make_async_copy(grad, grad_hbm, sems.at[1]),
        pltpu.make_async_copy(filter_grad, filter_grad_hbm, sems.at[2]),
    ]
    for copy in copies:
        copy.start()
    for copy in copies:
        copy.wait()


def per_device(patch_count, map_count, maps, cotangent, tiles, columns, filters):
    copies, chan, pix = maps.shape
    nb, slots, bs, _ = tiles.shape
    rows = copies * chan
    order = filters.shape[0]
    scale = 1.0 / math.sqrt(copies * map_count * pix * patch_count)
    hbm = pl.BlockSpec(memory_space=pltpu.HBM)
    vmem = pl.BlockSpec(memory_space=pltpu.VMEM)
    dma = pltpu.SemaphoreType.DMA
    field = pltpu.VMEM((nb + 2 * REACH, rows, bs), BF16)
    own = pltpu.VMEM((nb, rows, bs), BF16)
    wide = pltpu.VMEM((nb, rows, bs), F32)
    rim = pltpu.VMEM((2, REACH, rows, bs), BF16)
    lines = 8
    pieces = chan // lines
    packed = (chan, 2 * rows)
    piece = (lines, 2 * rows)
    pin = lambda x: pltpu.with_memory_space_constraint(x, pltpu.HBM)
    results = (
        jax.ShapeDtypeStruct((rows, pix), BF16),
        jax.ShapeDtypeStruct((rows, pix), BF16),
        jax.ShapeDtypeStruct((order, chan, chan), F32),
    )
    held = pl.pallas_call(
        functools.partial(kernel, patch_count, map_count, copies, scale),
        out_shape=results,
        in_specs=[hbm, hbm, hbm, hbm, hbm],
        out_specs=(vmem, vmem, vmem),
        scratch_shapes=[
            pltpu.SMEM((slots, nb), jnp.int32),
            pltpu.VMEM((order, chan, chan), BF16),
            pltpu.VMEM((nb, slots, bs, bs), BF16),
            pltpu.VMEM((nb, slots, bs, bs), BF16),
            field,
            field,
            own,
            own,
            wide,
            wide,
            rim,
            rim,
            rim,
            rim,
            pltpu.VMEM(packed, F32),
            pltpu.VMEM((patch_count,) + piece, F32),
            pltpu.VMEM((map_count,) + piece, F32),
            pltpu.VMEM(packed, F32),
            pltpu.VMEM((rows, 4 * rows), BF16),
            pltpu.VMEM((rows, 4 * rows), BF16),
            dma,
            dma,
            dma((nb,)),
            dma((nb,)),
            dma((nb,)),
            dma((2, 2, REACH)),
            dma((2, 2, REACH)),
            dma((2, 2)),
            dma((2, 2)),
            dma((patch_count - 1,)),
            dma((patch_count - 1,)),
            dma((map_count - 1,)),
            dma((map_count - 1,)),
            dma((pieces - 1,)),
            dma((pieces - 1,)),
        ],
        compiler_params=pltpu.CompilerParams(
            collective_id=0, has_side_effects=True, vmem_limit_bytes=40 * 1024 * 1024
        ),
    )(
        pin(maps.reshape(rows, pix)), pin(cotangent.reshape(rows, pix)), pin(tiles), pin(columns.T), pin(filters)
    )
    out, grad, filter_grad = pl.pallas_call(
        write,
        out_shape=results,
        in_specs=[vmem] * 3,
        out_specs=(hbm,) * 3,
        scratch_shapes=[dma((3,))],
        compiler_params=pltpu.CompilerParams(vmem_limit_bytes=4 * 1024 * 1024),
    )(*held)
    return out.reshape(copies, chan, pix), grad.reshape(copies, chan, pix), filter_grad


def solution(mesh):
    field = P("map", None, "patch")
    return jax.shard_map(
        functools.partial(per_device, mesh.shape["patch"], mesh.shape["map"]),
        mesh=mesh,
        in_specs=(field, field, P("patch", None, None, None), P("patch", None), P()),
        out_specs=(field, field, P()),
        check_vma=False,
    )
```

```python
import functools
import math

import jax
import jax.numpy as jnp
from jax import lax
from jax.experimental import pallas as pl
from jax.experimental.pallas import tpu as pltpu
from jax.sharding import PartitionSpec as P

REACH = 2
MESH = pl.DeviceIdType.MESH
F32 = jnp.float32
BF16 = jnp.bfloat16


def dot_nn(a, b):
    return lax.dot_general(a, b, (((1,), (0,)), ((), ())), preferred_element_type=F32)


def dot_nt(a, b):
    return lax.dot_general(a, b, (((1,), (1,)), ((), ())), preferred_element_type=F32)


def mixing(filters, copies):
    order, chan = filters.shape[0], filters.shape[1]
    zero = jnp.zeros((chan, chan), F32)
    adjoint, output = [], []
    for m in range(copies):
        adjoint.append([])
        output.append([])
        for k in list(range(order)) + [order - 1]:
            term = filters[k].astype(F32)
            for n in range(copies):
                adjoint[m].append(term if n == m else zero)
                output[m].append(term.T if n == m else zero)
    join = lambda rows: jnp.concatenate([jnp.concatenate(r, axis=1) for r in rows], axis=0).astype(BF16)
    return join(adjoint), join(output)


def kernel(
    patch_count,
    map_count,
    copies,
    scale,
    maps,
    cot,
    tiles_hbm,
    cols_hbm,
    filters_hbm,
    out,
    grad,
    filter_grad,
    cols,
    filters,
    tiles,
    x_zero,
    x_one,
    y_zero,
    y_one,
    window,
    to_left,
    to_right,
    from_left,
    from_right,
    terms_ref,
    sum_patch,
    sum_map,
    whole_ref,
    mix_out,
    mix_in,
    load_cols,
    load_filters,
    load_tile,
    load_x,
    load_y,
    halo_send,
    halo_recv,
    adj_send,
    adj_recv,
    patch_send,
    patch_recv,
    map_send,
    map_recv,
    gather_send,
    gather_recv,
):
    nb, _, bs, _ = tiles.shape
    reach = REACH
    me, my_map = lax.axis_index("patch"), lax.axis_index("map")
    left = lax.rem(me + patch_count - 1, patch_count)
    right = lax.rem(me + 1, patch_count)
    total = patch_count * nb

    half_nb = nb // 2

    def load_y_of(b):
        return pltpu.make_async_copy(cot.at[:, pl.ds(pl.multiple_of(b * bs, bs), bs)], y_zero.at[b], load_y.at[b])

    def load_x_of(b):
        return pltpu.make_async_copy(
            maps.at[:, pl.ds(pl.multiple_of(b * bs, bs), bs)], x_zero.at[reach + b], load_x.at[b]
        )

    def load_tile_of(b):
        return pltpu.make_async_copy(tiles_hbm.at[b], tiles.at[b], load_tile.at[b])

    load_c = pltpu.make_async_copy(cols_hbm, cols, load_cols)
    load_c.start()
    load_f = pltpu.make_async_copy(filters_hbm, filters, load_filters)
    load_f.start()

    @pl.loop(0, half_nb)
    def _(i):
        for b in (i, nb - 1 - i):
            load_y_of(b).start()
            load_tile_of(b).start()

    @pl.loop(0, half_nb)
    def _(i):
        for b in (i, nb - 1 - i):
            load_x_of(b).start()

    barrier = pltpu.get_barrier_semaphore()
    for d in range(1, patch_count):
        pl.semaphore_signal(barrier, inc=1, device_id=(lax.rem(me + d, patch_count), my_map), device_id_type=MESH)
    for d in range(1, map_count):
        pl.semaphore_signal(barrier, inc=1, device_id=(me, lax.rem(my_map + d, map_count)), device_id_type=MESH)

    load_f.wait()
    load_c.wait()
    mix_in[...], mix_out[...] = mixing(filters, copies)

    def near_left(b):
        return lax.rem(me * nb + b - cols[1, b] + total, total) == 1

    def near_right(b):
        return lax.rem(cols[2, b] - me * nb - b + total, total) == 1

    zero_rows = jnp.zeros(from_left.shape[2:], BF16)
    for turn in range(2):
        for i in range(reach, half_nb):
            from_left[turn, i] = zero_rows
            from_right[turn, half_nb - 1 - i] = zero_rows

    pl.semaphore_wait(barrier, patch_count + map_count - 2)

    def remote(src, dst, send_sem, recv_sem, patch, map_index):
        return pltpu.make_async_remote_copy(
            src_ref=src,
            dst_ref=dst,
            send_sem=send_sem,
            recv_sem=recv_sem,
            device_id=(patch, map_index),
            device_id_type=MESH,
        )

    def halo_copies(turn, source, field):
        return [
            copy
            for i in range(reach)
            for copy in (
                remote(source(i), field.at[reach + nb + i], halo_send.at[turn, 0, i], halo_recv.at[turn, 0, i], left, my_map),
                remote(
                    source(nb - reach + i), field.at[i], halo_send.at[turn, 1, i], halo_recv.at[turn, 1, i], right, my_map
                ),
            )
        ]

    def adjoint_copies(turn):
        return [
            remote(
                to_left.at[turn],
                from_right.at[turn, pl.ds(half_nb - reach, reach)],
                adj_send.at[turn, 0],
                adj_recv.at[turn, 0],
                left,
                my_map,
            ),
            remote(
                to_right.at[turn],
                from_left.at[turn, pl.ds(0, reach)],
                adj_send.at[turn, 1],
                adj_recv.at[turn, 1],
                right,
                my_map,
            ),
        ]

    def keep(flag, value):
        return jnp.where(flag, value, jnp.zeros_like(value))

    def adjoint(turn, w, copies_):
        window[...] = jnp.zeros_like(window)

        @pl.loop(0, half_nb)
        def _(i):
            pair = (i, nb - 1 - i)
            if turn == 0:
                for b in pair:
                    load_y_of(b).wait()
                    load_tile_of(b).wait()
            products = [[dot_nn(w[b], tiles[b, j]) for j in range(3)] for b in pair]
            for b, (own, before, after) in zip(pair, products):
                here = reach + b
                on_left, on_right = near_left(b), near_right(b)
                window[here] += own
                window[here - 1] += keep(on_left, before)
                window[here - 2] += keep(~on_left, before)
                window[here + 1] += keep(on_right, after)
                window[here + 2] += keep(~on_right, after)

            @pl.when(i == reach - 1)
            def _():
                for j in range(reach):
                    to_left[turn, j] = window[j].astype(BF16)
                    to_right[turn, j] = window[reach + nb + j].astype(BF16)
                for copy in copies_:
                    copy.start()

    def whole_adjoint(turn, i):
        return (
            window[reach + i] + from_left[turn, i].astype(F32),
            window[reach + nb - 1 - i] + from_right[turn, half_nb - 1 - i].astype(F32),
        )

    def forward(field, b):
        here = reach + b
        before = jnp.where(near_left(b), field[here - 1], field[here - 2])
        after = jnp.where(near_right(b), field[here + 1], field[here + 2])
        return dot_nt(field[here], tiles[b, 0]) + dot_nt(before, tiles[b, 1]) + dot_nt(after, tiles[b, 2])

    halo_zero = halo_copies(0, lambda b: maps.at[:, pl.ds(b * bs, bs)], x_zero)
    halo_one = halo_copies(1, lambda b: x_one.at[reach + b], x_one)
    adjoint_zero, adjoint_one = adjoint_copies(0), adjoint_copies(1)
    for copy in halo_zero:
        copy.start()
    adjoint(0, y_zero, adjoint_zero)

    @pl.loop(0, nb)
    def _(b):
        load_x_of(b).wait()

    for copy in halo_zero:
        copy.wait_recv()

    @pl.loop(0, half_nb)
    def _(i):
        pair = (i, nb - 1 - i)
        for b, value in zip(pair, [forward(x_zero, b) for b in pair]):
            x_one[reach + b] = value.astype(BF16)

        @pl.when(i == reach - 1)
        def _():
            for copy in halo_one:
                copy.start()

    for copy in adjoint_zero:
        copy.wait_recv()

    chan = filters.shape[1]
    edge = 2 * copies * chan

    def add_products(i, product):
        pair = (i, nb - 1 - i)
        for b, value in zip(pair, whole_adjoint(0, i)):
            y_one[b] = value.astype(BF16)
            rows = jnp.concatenate([x_zero[reach + b], x_one[reach + b]], axis=0)
            columns = jnp.concatenate([y_zero[b], y_one[b]], axis=0)
            product = product + dot_nt(rows, columns)
        return product

    product = lax.fori_loop(0, half_nb, add_products, jnp.zeros((edge, edge), F32))
    width = product.shape[1]
    half = copies * chan

    def fold(value):
        result = value[:chan]
        for m in range(1, copies):
            result = result + pltpu.roll(value[m * chan : (m + 1) * chan], width - m * chan, 1)
        return result

    with_zero, with_one = fold(product[:half]), fold(product[half:])
    lane = lax.broadcasted_iota(jnp.int32, (chan, width), 1)
    terms_ref[...] = jnp.where(
        lane < chan,
        with_zero,
        jnp.where(lane < 2 * chan, pltpu.roll(with_one, chan, 1), 2.0 * with_one - pltpu.roll(with_zero, half, 1)),
    )
    lines = sum_patch.shape[1]
    pieces = chan // lines

    def piece_of(device):
        return pl.ds(pl.multiple_of(lax.rem(device, pieces) * lines, lines), lines)

    sum_patch[me] = terms_ref[piece_of(me), :]
    over_patch = []
    for d in range(1, patch_count):
        peer = lax.rem(me + d, patch_count)
        over_patch.append(
            remote(
                terms_ref.at[piece_of(peer), :],
                sum_patch.at[me],
                patch_send.at[d - 1],
                patch_recv.at[d - 1],
                peer,
                my_map,
            )
        )
    for copy in over_patch:
        copy.start()

    adjoint(1, y_one, adjoint_one)
    for copy in over_patch:
        copy.wait_recv()
    partial = sum_patch[0]
    for i in range(1, patch_count):
        partial = partial + sum_patch[i]
    sum_map[my_map] = partial
    over_map = [
        remote(
            sum_map.at[my_map],
            sum_map.at[my_map],
            map_send.at[d - 1],
            map_recv.at[d - 1],
            me,
            lax.rem(my_map + d, map_count),
        )
        for d in range(1, map_count)
    ]
    for copy in over_map:
        copy.start()
    for copy in halo_one:
        copy.wait_recv()

    def place(b):
        return pl.ds(pl.multiple_of(b * bs, bs), bs)

    @pl.loop(0, half_nb)
    def _(i):
        pair = (i, nb - 1 - i)
        for b, applied in zip(pair, [forward(x_one, b) for b in pair]):
            first = x_zero[reach + b]
            x_two = (2.0 * applied - first.astype(F32)).astype(BF16)
            terms = jnp.concatenate([first, x_one[reach + b], x_two], axis=0)
            out[:, place(b)] = dot_nn(mix_out[:, : terms.shape[0]], terms).astype(BF16)

    for copy in over_map:
        copy.wait_recv()
    whole = sum_map[0]
    for i in range(1, map_count):
        whole = whole + sum_map[i]
    whole_ref[piece_of(me), :] = whole * scale
    base = me - lax.rem(me, pieces)
    gathered = []
    for d in range(1, pieces):
        gathered.append(
            remote(
                whole_ref.at[piece_of(me), :],
                whole_ref.at[piece_of(me), :],
                gather_send.at[d - 1],
                gather_recv.at[d - 1],
                base + lax.rem(me + d, pieces),
                my_map,
            )
        )
    for copy in gathered:
        copy.start()
    for copy in adjoint_one:
        copy.wait_recv()

    @pl.loop(0, half_nb)
    def _(i):
        pair = (i, nb - 1 - i)
        for b, value in zip(pair, whole_adjoint(1, i)):
            first = y_zero[b]
            y_two = 2.0 * value - first.astype(F32)
            coarse = y_two.astype(BF16)
            fine = (y_two - coarse.astype(F32)).astype(BF16)
            terms = jnp.concatenate([first, y_one[b], coarse, fine], axis=0)
            grad[:, place(b)] = dot_nn(mix_in[...], terms).astype(BF16)

    for copy in gathered:
        copy.wait_recv()
    whole = whole_ref[...]
    for k in range(filters.shape[0]):
        shifted = pltpu.roll(whole, width - k * chan, 1) if k else whole
        filter_grad[k] = shifted[:, :chan]
    for copy in halo_zero + halo_one + adjoint_zero + adjoint_one + over_patch + over_map + gathered:
        copy.wait_send()


def write(out, grad, filter_grad, out_hbm, grad_hbm, filter_grad_hbm, sems):
    copies = [
        pltpu.make_async_copy(out, out_hbm, sems.at[0]),
        pltpu.make_async_copy(grad, grad_hbm, sems.at[1]),
        pltpu.make_async_copy(filter_grad, filter_grad_hbm, sems.at[2]),
    ]
    for copy in copies:
        copy.start()
    for copy in copies:
        copy.wait()


def per_device(patch_count, map_count, maps, cotangent, tiles, columns, filters):
    copies, chan, pix = maps.shape
    nb, slots, bs, _ = tiles.shape
    rows = copies * chan
    order = filters.shape[0]
    scale = 1.0 / math.sqrt(copies * map_count * pix * patch_count)
    hbm = pl.BlockSpec(memory_space=pltpu.HBM)
    vmem = pl.BlockSpec(memory_space=pltpu.VMEM)
    dma = pltpu.SemaphoreType.DMA
    field = pltpu.VMEM((nb + 2 * REACH, rows, bs), BF16)
    own = pltpu.VMEM((nb, rows, bs), BF16)
    arrived = pltpu.VMEM((2, nb // 2, rows, bs), BF16)
    rim = pltpu.VMEM((2, REACH, rows, bs), BF16)
    lines = 8
    pieces = chan // lines
    packed = (chan, 2 * rows)
    piece = (lines, 2 * rows)
    pin = lambda x: pltpu.with_memory_space_constraint(x, pltpu.HBM)
    results = (
        jax.ShapeDtypeStruct((rows, pix), BF16),
        jax.ShapeDtypeStruct((rows, pix), BF16),
        jax.ShapeDtypeStruct((order, chan, chan), F32),
    )
    held = pl.pallas_call(
        functools.partial(kernel, patch_count, map_count, copies, scale),
        out_shape=results,
        in_specs=[hbm, hbm, hbm, hbm, hbm],
        out_specs=(vmem, vmem, vmem),
        scratch_shapes=[
            pltpu.SMEM((slots, nb), jnp.int32),
            pltpu.VMEM((order, chan, chan), BF16),
            pltpu.VMEM((nb, slots, bs, bs), BF16),
            field,
            field,
            own,
            own,
            pltpu.VMEM((nb + 2 * REACH, rows, bs), F32),
            rim,
            rim,
            arrived,
            arrived,
            pltpu.VMEM(packed, F32),
            pltpu.VMEM((patch_count,) + piece, F32),
            pltpu.VMEM((map_count,) + piece, F32),
            pltpu.VMEM(packed, F32),
            pltpu.VMEM((rows, 4 * rows), BF16),
            pltpu.VMEM((rows, 4 * rows), BF16),
            dma,
            dma,
            dma((nb,)),
            dma((nb,)),
            dma((nb,)),
            dma((2, 2, REACH)),
            dma((2, 2, REACH)),
            dma((2, 2)),
            dma((2, 2)),
            dma((patch_count - 1,)),
            dma((patch_count - 1,)),
            dma((map_count - 1,)),
            dma((map_count - 1,)),
            dma((pieces - 1,)),
            dma((pieces - 1,)),
        ],
        compiler_params=pltpu.CompilerParams(
            collective_id=0, has_side_effects=True, vmem_limit_bytes=40 * 1024 * 1024
        ),
    )(
        pin(maps.reshape(rows, pix)), pin(cotangent.reshape(rows, pix)), pin(tiles), pin(columns.T), pin(filters)
    )
    out, grad, filter_grad = pl.pallas_call(
        write,
        out_shape=results,
        in_specs=[vmem] * 3,
        out_specs=(hbm,) * 3,
        scratch_shapes=[dma((3,))],
        compiler_params=pltpu.CompilerParams(vmem_limit_bytes=4 * 1024 * 1024),
    )(*held)
    return out.reshape(copies, chan, pix), grad.reshape(copies, chan, pix), filter_grad


def solution(mesh):
    field = P("map", None, "patch")
    return jax.shard_map(
        functools.partial(per_device, mesh.shape["patch"], mesh.shape["map"]),
        mesh=mesh,
        in_specs=(field, field, P("patch", None, None, None), P("patch", None), P()),
        out_specs=(field, field, P()),
        check_vma=False,
    )
```

```python
import functools
import math

import jax
import jax.numpy as jnp
from jax import lax
from jax.experimental import pallas as pl
from jax.experimental.pallas import tpu as pltpu
from jax.sharding import PartitionSpec as P

REACH = 2
MESH = pl.DeviceIdType.MESH
F32 = jnp.float32
BF16 = jnp.bfloat16


def dot_nn(a, b):
    return lax.dot_general(a, b, (((1,), (0,)), ((), ())), preferred_element_type=F32)


def dot_nt(a, b):
    return lax.dot_general(a, b, (((1,), (1,)), ((), ())), preferred_element_type=F32)


def mixing(filters, copies):
    order, chan = filters.shape[0], filters.shape[1]
    zero = jnp.zeros((chan, chan), F32)
    adjoint, output = [], []
    for m in range(copies):
        adjoint.append([])
        output.append([])
        for k in list(range(order)) + [order - 1]:
            term = filters[k].astype(F32)
            for n in range(copies):
                adjoint[m].append(term if n == m else zero)
                output[m].append(term.T if n == m else zero)
    join = lambda rows: jnp.concatenate([jnp.concatenate(r, axis=1) for r in rows], axis=0).astype(BF16)
    return join(adjoint), join(output)


def kernel(
    patch_count,
    map_count,
    copies,
    scale,
    maps,
    cot,
    tiles_hbm,
    cols_hbm,
    filters_hbm,
    out,
    grad,
    filter_grad,
    cols,
    filters,
    tiles,
    turned_tiles,
    x_zero,
    x_one,
    y_zero,
    y_one,
    acc_x,
    acc_y,
    to_left,
    to_right,
    from_left,
    from_right,
    sum_patch,
    sum_map,
    mix_out,
    mix_in,
    load_cols,
    load_filters,
    load_tile,
    load_x,
    load_y,
    halo_send,
    halo_recv,
    adj_send,
    adj_recv,
    patch_send,
    patch_recv,
    map_send,
    map_recv,
):
    nb, _, bs, _ = tiles.shape
    reach = REACH
    me, my_map = lax.axis_index("patch"), lax.axis_index("map")
    left = lax.rem(me + patch_count - 1, patch_count)
    right = lax.rem(me + 1, patch_count)
    total = patch_count * nb
    low = list(range(reach))
    high = list(range(nb - reach, nb))
    middle = list(range(reach, nb - reach))
    edges = [b for pair in zip(low, reversed(high)) for b in pair]
    order = edges + middle

    barrier = pltpu.get_barrier_semaphore()
    for d in range(1, patch_count):
        pl.semaphore_signal(barrier, inc=1, device_id=(lax.rem(me + d, patch_count), my_map), device_id_type=MESH)
    for d in range(1, map_count):
        pl.semaphore_signal(barrier, inc=1, device_id=(me, lax.rem(my_map + d, map_count)), device_id_type=MESH)

    loads_y = [pltpu.make_async_copy(cot.at[:, pl.ds(b * bs, bs)], y_zero.at[b], load_y.at[b]) for b in range(nb)]
    loads_x = [pltpu.make_async_copy(maps.at[:, pl.ds(b * bs, bs)], x_zero.at[reach + b], load_x.at[b]) for b in range(nb)]
    loads_t = [pltpu.make_async_copy(tiles_hbm.at[b], tiles.at[b], load_tile.at[b]) for b in range(nb)]
    load_f = pltpu.make_async_copy(filters_hbm, filters, load_filters)
    load_f.start()
    load_c = pltpu.make_async_copy(cols_hbm, cols, load_cols)
    load_c.start()
    for b in order:
        loads_y[b].start()
        loads_t[b].start()
    for b in order:
        loads_x[b].start()

    def remote(src, dst, send_sem, recv_sem, patch, map_index):
        copy = pltpu.make_async_remote_copy(
            src_ref=src,
            dst_ref=dst,
            send_sem=send_sem,
            recv_sem=recv_sem,
            device_id=(patch, map_index),
            device_id_type=MESH,
        )
        copy.start()
        return copy

    sent = []

    def send_halo(turn, source, field):
        copies_ = []
        for i in range(reach):
            copies_.append(
                remote(source(i), field.at[reach + nb + i], halo_send.at[turn, 0, i], halo_recv.at[turn, 0, i], left, my_map)
            )
            copies_.append(
                remote(
                    source(nb - reach + i), field.at[i], halo_send.at[turn, 1, i], halo_recv.at[turn, 1, i], right, my_map
                )
            )
        sent.extend(copies_)
        return copies_

    def pick(flag, yes, no):
        return jnp.where(flag, yes, no)

    def keep(flag, value):
        return jnp.where(flag, value, jnp.zeros_like(value))

    def left_part(w, b):
        return dot_nn(w[b], tiles[b, 1])

    def right_part(w, b):
        return dot_nn(w[b], tiles[b, 2])

    def send_adjoint(turn, w):
        p1 = {b: left_part(w, b) for b in low}
        p2 = {b: right_part(w, b) for b in high}
        last = nb - 1
        to_left[turn, 1] = (keep(near_left[0], p1[0]) + keep(~near_left[1], p1[1])).astype(BF16)
        to_left[turn, 0] = keep(~near_left[0], p1[0]).astype(BF16)
        to_right[turn, 0] = (keep(near_right[last], p2[last]) + keep(~near_right[last - 1], p2[last - 1])).astype(BF16)
        to_right[turn, 1] = keep(~near_right[last], p2[last]).astype(BF16)
        copies_ = [
            remote(to_left.at[turn], from_right.at[turn], adj_send.at[turn, 0], adj_recv.at[turn, 0], left, my_map),
            remote(to_right.at[turn], from_left.at[turn], adj_send.at[turn, 1], adj_recv.at[turn, 1], right, my_map),
        ]
        sent.extend(copies_)
        return copies_, p1, p2

    def local_adjoint(w, p1, p2):
        p1, p2 = dict(p1), dict(p2)
        for b in range(nb):
            if b not in p1:
                p1[b] = left_part(w, b)
            if b not in p2:
                p2[b] = right_part(w, b)
        for t in range(nb):
            value = dot_nn(w[t], tiles[t, 0])
            if t + 1 < nb:
                value = value + keep(near_left[t + 1], p1[t + 1])
            if t + 2 < nb:
                value = value + keep(~near_left[t + 2], p1[t + 2])
            if t >= 1:
                value = value + keep(near_right[t - 1], p2[t - 1])
            if t >= 2:
                value = value + keep(~near_right[t - 2], p2[t - 2])
            acc_y[t] = value

    def whole_adjoint(turn, t):
        value = acc_y[t]
        if t < reach:
            value = value + from_left[turn, t].astype(F32)
        if t >= nb - reach:
            value = value + from_right[turn, t - (nb - reach)].astype(F32)
        return value

    def turned(field, b, slot):
        if field is x_zero:
            turned_tiles[b, slot] = tiles[b, slot].T
        return turned_tiles[b, slot]

    def own_term(field, b):
        return dot_nn(field[reach + b], turned(field, b, 0))

    def left_term(field, b):
        return dot_nn(pick(near_left[b], field[reach + b - 1], field[reach + b - 2]), turned(field, b, 1))

    def right_term(field, b):
        return dot_nn(pick(near_right[b], field[reach + b + 1], field[reach + b + 2]), turned(field, b, 2))

    def inner_forward(field, b):
        value = own_term(field, b)
        if b >= reach:
            value = value + left_term(field, b)
        if b < nb - reach:
            value = value + right_term(field, b)
        return value

    def rest_forward(field, b):
        return left_term(field, b) if b < reach else right_term(field, b)

    pl.semaphore_wait(barrier, patch_count + map_count - 2)
    halo = send_halo(0, lambda b: maps.at[:, pl.ds(b * bs, bs)], x_zero)
    load_c.wait()
    near_left = [lax.rem(me * nb + b - cols[1, b] + total, total) == 1 for b in range(nb)]
    near_right = [lax.rem(cols[2, b] - me * nb - b + total, total) == 1 for b in range(nb)]
    for b in edges:
        loads_y[b].wait()
        loads_t[b].wait()
    adj, p1, p2 = send_adjoint(0, y_zero)
    load_f.wait()
    mix_in[...], mix_out[...] = mixing(filters, copies)
    for b in middle:
        loads_y[b].wait()
        loads_t[b].wait()
    for b in range(nb):
        loads_x[b].wait()
    for b in edges:
        acc_x[b] = inner_forward(x_zero, b)
    for b in middle:
        x_one[reach + b] = inner_forward(x_zero, b).astype(BF16)
    for copy in halo:
        copy.wait_recv()
    for b in edges:
        x_one[reach + b] = (acc_x[b] + rest_forward(x_zero, b)).astype(BF16)
    halo = send_halo(1, lambda b: x_one.at[reach + b], x_one)
    local_adjoint(y_zero, p1, p2)
    for copy in adj:
        copy.wait_recv()
    for b in range(nb):
        y_one[b] = whole_adjoint(0, b).astype(BF16)
    adj, p1, p2 = send_adjoint(1, y_one)

    chan = filters.shape[1]
    product = None
    for b in range(nb):
        rows = jnp.concatenate([x_zero[reach + b], x_one[reach + b]], axis=0)
        columns = jnp.concatenate([y_zero[b], y_one[b]], axis=0)
        term = dot_nt(rows, columns)
        product = term if product is None else product + term
    width = product.shape[1]
    half = copies * chan

    def fold(value):
        result = value[:chan]
        for m in range(1, copies):
            result = result + pltpu.roll(value[m * chan : (m + 1) * chan], width - m * chan, 1)
        return result

    with_zero, with_one = fold(product[:half]), fold(product[half:])
    lane = lax.broadcasted_iota(jnp.int32, (chan, width), 1)
    packed = jnp.where(
        lane < chan,
        with_zero,
        jnp.where(lane < 2 * chan, pltpu.roll(with_one, chan, 1), 2.0 * with_one - pltpu.roll(with_zero, half, 1)),
    )
    sum_patch[me] = packed
    over_patch = [
        remote(
            sum_patch.at[me],
            sum_patch.at[me],
            patch_send.at[d - 1],
            patch_recv.at[d - 1],
            lax.rem(me + d, patch_count),
            my_map,
        )
        for d in range(1, patch_count)
    ]
    sent.extend(over_patch)

    local_adjoint(y_one, p1, p2)
    for b in edges:
        acc_x[b] = inner_forward(x_one, b)

    def write_output(b, applied):
        first = x_zero[reach + b]
        x_two = (2.0 * applied - first.astype(F32)).astype(BF16)
        terms = jnp.concatenate([first, x_one[reach + b], x_two], axis=0)
        out[:, b * bs : (b + 1) * bs] = dot_nn(mix_out[:, : terms.shape[0]], terms).astype(BF16)

    def write_grad(b):
        first = y_zero[b]
        y_two = 2.0 * whole_adjoint(1, b) - first.astype(F32)
        coarse = y_two.astype(BF16)
        fine = (y_two - coarse.astype(F32)).astype(BF16)
        terms = jnp.concatenate([first, y_one[b], coarse, fine], axis=0)
        grad[:, b * bs : (b + 1) * bs] = dot_nn(mix_in[...], terms).astype(BF16)

    for copy in over_patch:
        copy.wait_recv()
    partial = sum_patch[0]
    for i in range(1, patch_count):
        partial = partial + sum_patch[i]
    sum_map[my_map] = partial
    over_map = [
        remote(
            sum_map.at[my_map],
            sum_map.at[my_map],
            map_send.at[d - 1],
            map_recv.at[d - 1],
            me,
            lax.rem(my_map + d, map_count),
        )
        for d in range(1, map_count)
    ]
    sent.extend(over_map)
    for b in middle:
        write_output(b, inner_forward(x_one, b))
        write_grad(b)
    for copy in halo:
        copy.wait_recv()
    for b in edges:
        write_output(b, acc_x[b] + rest_forward(x_one, b))
    for copy in adj:
        copy.wait_recv()
    for b in edges:
        write_grad(b)
    for copy in over_map:
        copy.wait_recv()
    whole = sum_map[0]
    for i in range(1, map_count):
        whole = whole + sum_map[i]
    whole = whole * scale
    for k in range(filters.shape[0]):
        shifted = pltpu.roll(whole, width - k * chan, 1) if k else whole
        filter_grad[k] = shifted[:, :chan]
    for copy in sent:
        copy.wait_send()


def write(out, grad, filter_grad, out_hbm, grad_hbm, filter_grad_hbm, sems):
    copies = [
        pltpu.make_async_copy(out, out_hbm, sems.at[0]),
        pltpu.make_async_copy(grad, grad_hbm, sems.at[1]),
        pltpu.make_async_copy(filter_grad, filter_grad_hbm, sems.at[2]),
    ]
    for copy in copies:
        copy.start()
    for copy in copies:
        copy.wait()


def per_device(patch_count, map_count, maps, cotangent, tiles, columns, filters):
    copies, chan, pix = maps.shape
    nb, slots, bs, _ = tiles.shape
    rows = copies * chan
    order = filters.shape[0]
    scale = 1.0 / math.sqrt(copies * map_count * pix * patch_count)
    hbm = pl.BlockSpec(memory_space=pltpu.HBM)
    vmem = pl.BlockSpec(memory_space=pltpu.VMEM)
    dma = pltpu.SemaphoreType.DMA
    field = pltpu.VMEM((nb + 2 * REACH, rows, bs), BF16)
    own = pltpu.VMEM((nb, rows, bs), BF16)
    wide = pltpu.VMEM((nb, rows, bs), F32)
    rim = pltpu.VMEM((2, REACH, rows, bs), BF16)
    packed = (chan, 2 * rows)
    pin = lambda x: pltpu.with_memory_space_constraint(x, pltpu.HBM)
    results = (
        jax.ShapeDtypeStruct((rows, pix), BF16),
        jax.ShapeDtypeStruct((rows, pix), BF16),
        jax.ShapeDtypeStruct((order, chan, chan), F32),
    )
    held = pl.pallas_call(
        functools.partial(kernel, patch_count, map_count, copies, scale),
        out_shape=results,
        in_specs=[hbm, hbm, hbm, hbm, hbm],
        out_specs=(vmem, vmem, vmem),
        scratch_shapes=[
            pltpu.SMEM((slots, nb), jnp.int32),
            pltpu.VMEM((order, chan, chan), BF16),
            pltpu.VMEM((nb, slots, bs, bs), BF16),
            pltpu.VMEM((nb, slots, bs, bs), BF16),
            field,
            field,
            own,
            own,
            wide,
            wide,
            rim,
            rim,
            rim,
            rim,
            pltpu.VMEM((patch_count,) + packed, F32),
            pltpu.VMEM((map_count,) + packed, F32),
            pltpu.VMEM((rows, 4 * rows), BF16),
            pltpu.VMEM((rows, 4 * rows), BF16),
            dma,
            dma,
            dma((nb,)),
            dma((nb,)),
            dma((nb,)),
            dma((2, 2, REACH)),
            dma((2, 2, REACH)),
            dma((2, 2)),
            dma((2, 2)),
            dma((patch_count - 1,)),
            dma((patch_count - 1,)),
            dma((map_count - 1,)),
            dma((map_count - 1,)),
        ],
        compiler_params=pltpu.CompilerParams(
            collective_id=0, has_side_effects=True, vmem_limit_bytes=40 * 1024 * 1024
        ),
    )(
        pin(maps.reshape(rows, pix)), pin(cotangent.reshape(rows, pix)), pin(tiles), pin(columns.T), pin(filters)
    )
    out, grad, filter_grad = pl.pallas_call(
        write,
        out_shape=results,
        in_specs=[vmem] * 3,
        out_specs=(hbm,) * 3,
        scratch_shapes=[dma((3,))],
        compiler_params=pltpu.CompilerParams(vmem_limit_bytes=4 * 1024 * 1024),
    )(*held)
    return out.reshape(copies, chan, pix), grad.reshape(copies, chan, pix), filter_grad


def solution(mesh):
    field = P("map", None, "patch")
    return jax.shard_map(
        functools.partial(per_device, mesh.shape["patch"], mesh.shape["map"]),
        mesh=mesh,
        in_specs=(field, field, P("patch", None, None, None), P("patch", None), P()),
        out_specs=(field, field, P()),
        check_vma=False,
    )
```

```python
import functools
import math

import jax
import jax.numpy as jnp
from jax import lax
from jax.experimental import pallas as pl
from jax.experimental.pallas import tpu as pltpu
from jax.sharding import PartitionSpec as P

REACH = 2
MESH = pl.DeviceIdType.MESH
F32 = jnp.float32
BF16 = jnp.bfloat16


def dot_nn(a, b):
    return lax.dot_general(a, b, (((1,), (0,)), ((), ())), preferred_element_type=F32)


def dot_nt(a, b):
    return lax.dot_general(a, b, (((1,), (1,)), ((), ())), preferred_element_type=F32)


def mixing(filters, copies):
    order, chan = filters.shape[0], filters.shape[1]
    zero = jnp.zeros((chan, chan), F32)
    adjoint, output = [], []
    for m in range(copies):
        adjoint.append([])
        output.append([])
        for k in list(range(order)) + [order - 1]:
            term = filters[k].astype(F32)
            for n in range(copies):
                adjoint[m].append(term if n == m else zero)
                output[m].append(term.T if n == m else zero)
    join = lambda rows: jnp.concatenate([jnp.concatenate(r, axis=1) for r in rows], axis=0).astype(BF16)
    return join(adjoint), join(output)


def kernel(
    patch_count,
    map_count,
    copies,
    scale,
    maps,
    cot,
    tiles_hbm,
    cols_hbm,
    filters_hbm,
    out,
    grad,
    filter_grad,
    cols,
    filters,
    tiles,
    turned_tiles,
    x_zero,
    x_one,
    y_zero,
    y_one,
    acc_x,
    acc_y,
    to_left,
    to_right,
    from_left,
    from_right,
    early_patch,
    early_map,
    late_patch,
    late_map,
    mix_out,
    mix_in,
    load_cols,
    load_filters,
    load_tile,
    load_x,
    load_y,
    halo_send,
    halo_recv,
    adj_send,
    adj_recv,
    patch_send,
    patch_recv,
    map_send,
    map_recv,
):
    nb, _, bs, _ = tiles.shape
    reach = REACH
    me, my_map = lax.axis_index("patch"), lax.axis_index("map")
    left = lax.rem(me + patch_count - 1, patch_count)
    right = lax.rem(me + 1, patch_count)
    total = patch_count * nb
    low = list(range(reach))
    high = list(range(nb - reach, nb))
    middle = list(range(reach, nb - reach))
    edges = [b for pair in zip(low, reversed(high)) for b in pair]
    order = edges + middle

    barrier = pltpu.get_barrier_semaphore()
    for d in range(1, patch_count):
        pl.semaphore_signal(barrier, inc=1, device_id=(lax.rem(me + d, patch_count), my_map), device_id_type=MESH)
    for d in range(1, map_count):
        pl.semaphore_signal(barrier, inc=1, device_id=(me, lax.rem(my_map + d, map_count)), device_id_type=MESH)

    loads_y = [pltpu.make_async_copy(cot.at[:, pl.ds(b * bs, bs)], y_zero.at[b], load_y.at[b]) for b in range(nb)]
    loads_x = [pltpu.make_async_copy(maps.at[:, pl.ds(b * bs, bs)], x_zero.at[reach + b], load_x.at[b]) for b in range(nb)]
    loads_t = [pltpu.make_async_copy(tiles_hbm.at[b], tiles.at[b], load_tile.at[b]) for b in range(nb)]
    load_f = pltpu.make_async_copy(filters_hbm, filters, load_filters)
    load_f.start()
    load_c = pltpu.make_async_copy(cols_hbm, cols, load_cols)
    load_c.start()
    for b in order:
        loads_y[b].start()
        loads_t[b].start()
    for b in order:
        loads_x[b].start()

    def remote(src, dst, send_sem, recv_sem, patch, map_index):
        copy = pltpu.make_async_remote_copy(
            src_ref=src,
            dst_ref=dst,
            send_sem=send_sem,
            recv_sem=recv_sem,
            device_id=(patch, map_index),
            device_id_type=MESH,
        )
        copy.start()
        return copy

    sent = []

    def send_maps():
        copies_ = []
        for i in range(reach):
            copies_.append(
                remote(
                    maps.at[:, pl.ds(i * bs, bs)],
                    x_zero.at[reach + nb + i],
                    halo_send.at[0, 0, i],
                    halo_recv.at[0, 0, i],
                    left,
                    my_map,
                )
            )
            copies_.append(
                remote(
                    maps.at[:, pl.ds((nb - reach + i) * bs, bs)],
                    x_zero.at[i],
                    halo_send.at[0, 1, i],
                    halo_recv.at[0, 1, i],
                    right,
                    my_map,
                )
            )
        sent.extend(copies_)
        return copies_

    def send_x_one():
        copies_ = [
            remote(
                x_one.at[pl.ds(reach, reach)],
                x_one.at[pl.ds(reach + nb, reach)],
                halo_send.at[1, 0, 0],
                halo_recv.at[1, 0, 0],
                left,
                my_map,
            ),
            remote(
                x_one.at[pl.ds(nb, reach)],
                x_one.at[pl.ds(0, reach)],
                halo_send.at[1, 1, 0],
                halo_recv.at[1, 1, 0],
                right,
                my_map,
            ),
        ]
        sent.extend(copies_)
        return copies_

    chan = filters.shape[1]
    half = copies * chan
    width = 2 * half

    def fold(value):
        result = value[:chan]
        for m in range(1, copies):
            result = result + pltpu.roll(value[m * chan : (m + 1) * chan], width - m * chan, 1)
        return result

    def lanes(parts):
        lane = lax.broadcasted_iota(jnp.int32, parts[0].shape, 1)
        return jnp.where(
            lane < chan,
            parts[0],
            jnp.where(
                lane < half,
                pltpu.roll(parts[1], chan, 1),
                jnp.where(lane < half + chan, parts[2], pltpu.roll(parts[3], chan, 1)),
            ),
        )

    def start_patch(stage, buffer, value):
        buffer[me] = value
        copies_ = [
            remote(
                buffer.at[me],
                buffer.at[me],
                patch_send.at[stage, d - 1],
                patch_recv.at[stage, d - 1],
                lax.rem(me + d, patch_count),
                my_map,
            )
            for d in range(1, patch_count)
        ]
        sent.extend(copies_)
        return copies_

    def total_of(buffer, count, copies_):
        for copy in copies_:
            copy.wait_recv()
        result = buffer[0]
        for i in range(1, count):
            result = result + buffer[i]
        return result

    def start_map(stage, buffer, value):
        buffer[my_map] = value
        copies_ = [
            remote(
                buffer.at[my_map],
                buffer.at[my_map],
                map_send.at[stage, d - 1],
                map_recv.at[stage, d - 1],
                me,
                lax.rem(my_map + d, map_count),
            )
            for d in range(1, map_count)
        ]
        sent.extend(copies_)
        return copies_

    def pick(flag, yes, no):
        return jnp.where(flag, yes, no)

    def keep(flag, value):
        return jnp.where(flag, value, jnp.zeros_like(value))

    def left_part(w, b):
        return dot_nn(w[b], tiles[b, 1])

    def right_part(w, b):
        return dot_nn(w[b], tiles[b, 2])

    def send_adjoint(turn, w):
        p1 = {b: left_part(w, b) for b in low}
        p2 = {b: right_part(w, b) for b in high}
        last = nb - 1
        to_left[turn, 1] = (keep(near_left[0], p1[0]) + keep(~near_left[1], p1[1])).astype(BF16)
        to_left[turn, 0] = keep(~near_left[0], p1[0]).astype(BF16)
        to_right[turn, 0] = (keep(near_right[last], p2[last]) + keep(~near_right[last - 1], p2[last - 1])).astype(BF16)
        to_right[turn, 1] = keep(~near_right[last], p2[last]).astype(BF16)
        copies_ = [
            remote(to_left.at[turn], from_right.at[turn], adj_send.at[turn, 0], adj_recv.at[turn, 0], left, my_map),
            remote(to_right.at[turn], from_left.at[turn], adj_send.at[turn, 1], adj_recv.at[turn, 1], right, my_map),
        ]
        sent.extend(copies_)
        return copies_, p1, p2

    def local_adjoint(w, p1, p2):
        p1, p2 = dict(p1), dict(p2)
        for b in range(nb):
            if b not in p1:
                p1[b] = left_part(w, b)
            if b not in p2:
                p2[b] = right_part(w, b)
        for t in range(nb):
            value = dot_nn(w[t], tiles[t, 0])
            if t + 1 < nb:
                value = value + keep(near_left[t + 1], p1[t + 1])
            if t + 2 < nb:
                value = value + keep(~near_left[t + 2], p1[t + 2])
            if t >= 1:
                value = value + keep(near_right[t - 1], p2[t - 1])
            if t >= 2:
                value = value + keep(~near_right[t - 2], p2[t - 2])
            acc_y[t] = value

    def whole_adjoint(turn, t):
        value = acc_y[t]
        if t < reach:
            value = value + from_left[turn, t].astype(F32)
        if t >= nb - reach:
            value = value + from_right[turn, t - (nb - reach)].astype(F32)
        return value

    def turned(field, b, slot):
        if field is x_zero:
            turned_tiles[b, slot] = tiles[b, slot].T
        return turned_tiles[b, slot]

    def own_term(field, b):
        return dot_nn(field[reach + b], turned(field, b, 0))

    def left_term(field, b):
        return dot_nn(pick(near_left[b], field[reach + b - 1], field[reach + b - 2]), turned(field, b, 1))

    def right_term(field, b):
        return dot_nn(pick(near_right[b], field[reach + b + 1], field[reach + b + 2]), turned(field, b, 2))

    def inner_forward(field, b):
        value = own_term(field, b)
        if b >= reach:
            value = value + left_term(field, b)
        if b < nb - reach:
            value = value + right_term(field, b)
        return value

    def rest_forward(field, b):
        return left_term(field, b) if b < reach else right_term(field, b)

    pl.semaphore_wait(barrier, patch_count + map_count - 2)
    halo = send_maps()
    load_c.wait()
    near_left = [lax.rem(me * nb + b - cols[1, b] + total, total) == 1 for b in range(nb)]
    near_right = [lax.rem(cols[2, b] - me * nb - b + total, total) == 1 for b in range(nb)]
    for b in edges:
        loads_y[b].wait()
        loads_t[b].wait()
    adj, p1, p2 = send_adjoint(0, y_zero)
    load_f.wait()
    mix_in[...], mix_out[...] = mixing(filters, copies)
    for b in middle:
        loads_y[b].wait()
        loads_t[b].wait()
    for b in range(nb):
        loads_x[b].wait()
    for b in edges:
        acc_x[b] = inner_forward(x_zero, b)
    for b in middle:
        x_one[reach + b] = inner_forward(x_zero, b).astype(BF16)
    for copy in halo:
        copy.wait_recv()
    for b in edges:
        x_one[reach + b] = (acc_x[b] + rest_forward(x_zero, b)).astype(BF16)
    halo = send_x_one()

    product = None
    for b in range(nb):
        rows = jnp.concatenate([x_zero[reach + b], x_one[reach + b]], axis=0)
        term = dot_nt(rows, jnp.concatenate([y_zero[b], y_zero[b]], axis=0))
        product = term if product is None else product + term
    zeroth, first_order = fold(product[:half]), fold(product[half:])
    mid = chan // 2
    early = start_patch(0, early_patch, lanes([zeroth[:mid], zeroth[mid:], first_order[:mid], first_order[mid:]]))

    local_adjoint(y_zero, p1, p2)
    for copy in adj:
        copy.wait_recv()
    product = None
    for b in range(nb):
        y_one[b] = whole_adjoint(0, b).astype(BF16)
        term = dot_nt(x_one[reach + b], jnp.concatenate([y_one[b], y_one[b]], axis=0))
        product = term if product is None else product + term
    second = fold(product)
    quarter = chan // 4
    late = start_patch(1, late_patch, lanes([second[i * quarter : (i + 1) * quarter] for i in range(4)]))

    adj, p1, p2 = send_adjoint(1, y_one)
    early = start_map(0, early_map, total_of(early_patch, patch_count, early))
    for b in edges:
        acc_x[b] = inner_forward(x_one, b)

    def write_output(b, applied):
        first = x_zero[reach + b]
        x_two = (2.0 * applied - first.astype(F32)).astype(BF16)
        terms = jnp.concatenate([first, x_one[reach + b], x_two], axis=0)
        out[:, b * bs : (b + 1) * bs] = dot_nn(mix_out[:, : terms.shape[0]], terms).astype(BF16)

    def write_grad(b):
        first = y_zero[b]
        y_two = 2.0 * whole_adjoint(1, b) - first.astype(F32)
        coarse = y_two.astype(BF16)
        fine = (y_two - coarse.astype(F32)).astype(BF16)
        terms = jnp.concatenate([first, y_one[b], coarse, fine], axis=0)
        grad[:, b * bs : (b + 1) * bs] = dot_nn(mix_in[...], terms).astype(BF16)

    late = start_map(1, late_map, total_of(late_patch, patch_count, late))
    local_adjoint(y_one, p1, p2)
    for b in middle:
        write_output(b, inner_forward(x_one, b))
        write_grad(b)
    for copy in halo:
        copy.wait_recv()
    for b in edges:
        write_output(b, acc_x[b] + rest_forward(x_one, b))
    for copy in adj:
        copy.wait_recv()
    for b in edges:
        write_grad(b)
    whole = total_of(early_map, map_count, early) * scale
    shifted = [pltpu.roll(whole, width - i * chan, 1)[:, :chan] if i else whole[:, :chan] for i in range(4)]
    filter_grad[0, :mid], filter_grad[0, mid:] = shifted[0], shifted[1]
    filter_grad[1, :mid], filter_grad[1, mid:] = shifted[2], shifted[3]
    whole = total_of(late_map, map_count, late) * scale
    for i in range(4):
        lines = slice(i * quarter, (i + 1) * quarter)
        part = pltpu.roll(whole, width - i * chan, 1)[:, :chan] if i else whole[:, :chan]
        filter_grad[2, lines] = 2.0 * part - filter_grad[0, lines]
    for copy in sent:
        copy.wait_send()


def write(out, grad, filter_grad, out_hbm, grad_hbm, filter_grad_hbm, sems):
    copies = [
        pltpu.make_async_copy(out, out_hbm, sems.at[0]),
        pltpu.make_async_copy(grad, grad_hbm, sems.at[1]),
        pltpu.make_async_copy(filter_grad, filter_grad_hbm, sems.at[2]),
    ]
    for copy in copies:
        copy.start()
    for copy in copies:
        copy.wait()


def per_device(patch_count, map_count, maps, cotangent, tiles, columns, filters):
    copies, chan, pix = maps.shape
    nb, slots, bs, _ = tiles.shape
    rows = copies * chan
    order = filters.shape[0]
    scale = 1.0 / math.sqrt(copies * map_count * pix * patch_count)
    hbm = pl.BlockSpec(memory_space=pltpu.HBM)
    vmem = pl.BlockSpec(memory_space=pltpu.VMEM)
    dma = pltpu.SemaphoreType.DMA
    field = pltpu.VMEM((nb + 2 * REACH, rows, bs), BF16)
    own = pltpu.VMEM((nb, rows, bs), BF16)
    wide = pltpu.VMEM((nb, rows, bs), F32)
    rim = pltpu.VMEM((2, REACH, rows, bs), BF16)
    pin = lambda x: pltpu.with_memory_space_constraint(x, pltpu.HBM)
    results = (
        jax.ShapeDtypeStruct((rows, pix), BF16),
        jax.ShapeDtypeStruct((rows, pix), BF16),
        jax.ShapeDtypeStruct((order, chan, chan), F32),
    )
    held = pl.pallas_call(
        functools.partial(kernel, patch_count, map_count, copies, scale),
        out_shape=results,
        in_specs=[hbm, hbm, hbm, hbm, hbm],
        out_specs=(vmem, vmem, vmem),
        scratch_shapes=[
            pltpu.SMEM((slots, nb), jnp.int32),
            pltpu.VMEM((order, chan, chan), BF16),
            pltpu.VMEM((nb, slots, bs, bs), BF16),
            pltpu.VMEM((nb, slots, bs, bs), BF16),
            field,
            field,
            own,
            own,
            wide,
            wide,
            rim,
            rim,
            rim,
            rim,
            pltpu.VMEM((patch_count, chan // 2, 2 * rows), F32),
            pltpu.VMEM((map_count, chan // 2, 2 * rows), F32),
            pltpu.VMEM((patch_count, chan // 4, 2 * rows), F32),
            pltpu.VMEM((map_count, chan // 4, 2 * rows), F32),
            pltpu.VMEM((rows, 4 * rows), BF16),
            pltpu.VMEM((rows, 4 * rows), BF16),
            dma,
            dma,
            dma((nb,)),
            dma((nb,)),
            dma((nb,)),
            dma((2, 2, REACH)),
            dma((2, 2, REACH)),
            dma((2, 2)),
            dma((2, 2)),
            dma((2, patch_count - 1)),
            dma((2, patch_count - 1)),
            dma((2, map_count - 1)),
            dma((2, map_count - 1)),
        ],
        compiler_params=pltpu.CompilerParams(
            collective_id=0, has_side_effects=True, vmem_limit_bytes=40 * 1024 * 1024
        ),
    )(
        pin(maps.reshape(rows, pix)), pin(cotangent.reshape(rows, pix)), pin(tiles), pin(columns.T), pin(filters)
    )
    out, grad, filter_grad = pl.pallas_call(
        write,
        out_shape=results,
        in_specs=[vmem] * 3,
        out_specs=(hbm,) * 3,
        scratch_shapes=[dma((3,))],
        compiler_params=pltpu.CompilerParams(vmem_limit_bytes=4 * 1024 * 1024),
    )(*held)
    return out.reshape(copies, chan, pix), grad.reshape(copies, chan, pix), filter_grad


def solution(mesh):
    field = P("map", None, "patch")
    return jax.shard_map(
        functools.partial(per_device, mesh.shape["patch"], mesh.shape["map"]),
        mesh=mesh,
        in_specs=(field, field, P("patch", None, None, None), P("patch", None), P()),
        out_specs=(field, field, P()),
        check_vma=False,
    )
```

```python
import functools
import math

import jax
import jax.numpy as jnp
from jax import lax
from jax.experimental import pallas as pl
from jax.experimental.pallas import tpu as pltpu
from jax.sharding import PartitionSpec as P

REACH = 2
MESH = pl.DeviceIdType.MESH
F32 = jnp.float32
BF16 = jnp.bfloat16


def dot_nn(a, b):
    return lax.dot_general(a, b, (((1,), (0,)), ((), ())), preferred_element_type=F32)


def dot_nt(a, b):
    return lax.dot_general(a, b, (((1,), (1,)), ((), ())), preferred_element_type=F32)


def mixing(filters, copies):
    order, chan = filters.shape[0], filters.shape[1]
    zero = jnp.zeros((chan, chan), F32)
    adjoint, output = [], []
    for m in range(copies):
        adjoint.append([])
        output.append([])
        for k in list(range(order)) + [order - 1]:
            term = filters[k].astype(F32)
            for n in range(copies):
                adjoint[m].append(term if n == m else zero)
                output[m].append(term.T if n == m else zero)
    join = lambda rows: jnp.concatenate([jnp.concatenate(r, axis=1) for r in rows], axis=0).astype(BF16)
    return join(adjoint), join(output)


def kernel(
    patch_count,
    map_count,
    copies,
    scale,
    maps,
    cot,
    tiles_hbm,
    cols_hbm,
    filters_hbm,
    out,
    grad,
    filter_grad,
    cols,
    filters,
    tiles,
    turned_tiles,
    x_zero,
    x_one,
    y_zero,
    y_one,
    acc_x,
    acc_y,
    to_left,
    to_right,
    from_left,
    from_right,
    early_patch,
    early_map,
    late_patch,
    late_map,
    mix_out,
    mix_in,
    load_cols,
    load_filters,
    load_tile,
    load_x,
    load_y,
    halo_send,
    halo_recv,
    adj_send,
    adj_recv,
    patch_send,
    patch_recv,
    map_send,
    map_recv,
):
    nb, _, bs, _ = tiles.shape
    reach = REACH
    me, my_map = lax.axis_index("patch"), lax.axis_index("map")
    left = lax.rem(me + patch_count - 1, patch_count)
    right = lax.rem(me + 1, patch_count)
    total = patch_count * nb
    low = list(range(reach))
    high = list(range(nb - reach, nb))
    middle = list(range(reach, nb - reach))
    edges = [b for pair in zip(low, reversed(high)) for b in pair]
    order = edges + middle

    barrier = pltpu.get_barrier_semaphore()
    for d in range(1, patch_count):
        pl.semaphore_signal(barrier, inc=1, device_id=(lax.rem(me + d, patch_count), my_map), device_id_type=MESH)
    for d in range(1, map_count):
        pl.semaphore_signal(barrier, inc=1, device_id=(me, lax.rem(my_map + d, map_count)), device_id_type=MESH)

    loads_y = [pltpu.make_async_copy(cot.at[:, pl.ds(b * bs, bs)], y_zero.at[b], load_y.at[b]) for b in range(nb)]
    loads_x = [pltpu.make_async_copy(maps.at[:, pl.ds(b * bs, bs)], x_zero.at[reach + b], load_x.at[b]) for b in range(nb)]
    loads_t = [pltpu.make_async_copy(tiles_hbm.at[b], tiles.at[b], load_tile.at[b]) for b in range(nb)]
    load_f = pltpu.make_async_copy(filters_hbm, filters, load_filters)
    load_f.start()
    load_c = pltpu.make_async_copy(cols_hbm, cols, load_cols)
    load_c.start()
    for b in order:
        loads_y[b].start()
        loads_t[b].start()
    for b in order:
        loads_x[b].start()

    def remote(src, dst, send_sem, recv_sem, patch, map_index):
        copy = pltpu.make_async_remote_copy(
            src_ref=src,
            dst_ref=dst,
            send_sem=send_sem,
            recv_sem=recv_sem,
            device_id=(patch, map_index),
            device_id_type=MESH,
        )
        copy.start()
        return copy

    sent = []

    def send_maps():
        copies_ = []
        for i in range(reach):
            copies_.append(
                remote(
                    maps.at[:, pl.ds(i * bs, bs)],
                    x_zero.at[reach + nb + i],
                    halo_send.at[0, 0, i],
                    halo_recv.at[0, 0, i],
                    left,
                    my_map,
                )
            )
            copies_.append(
                remote(
                    maps.at[:, pl.ds((nb - reach + i) * bs, bs)],
                    x_zero.at[i],
                    halo_send.at[0, 1, i],
                    halo_recv.at[0, 1, i],
                    right,
                    my_map,
                )
            )
        sent.extend(copies_)
        return copies_

    def send_x_one():
        copies_ = [
            remote(
                x_one.at[pl.ds(reach, reach)],
                x_one.at[pl.ds(reach + nb, reach)],
                halo_send.at[1, 0, 0],
                halo_recv.at[1, 0, 0],
                left,
                my_map,
            ),
            remote(
                x_one.at[pl.ds(nb, reach)],
                x_one.at[pl.ds(0, reach)],
                halo_send.at[1, 1, 0],
                halo_recv.at[1, 1, 0],
                right,
                my_map,
            ),
        ]
        sent.extend(copies_)
        return copies_

    chan = filters.shape[1]
    half = copies * chan
    width = 2 * half

    def fold(value):
        result = value[:chan]
        for m in range(1, copies):
            result = result + pltpu.roll(value[m * chan : (m + 1) * chan], width - m * chan, 1)
        return result

    def lanes(parts):
        lane = lax.broadcasted_iota(jnp.int32, parts[0].shape, 1)
        return jnp.where(
            lane < chan,
            parts[0],
            jnp.where(
                lane < half,
                pltpu.roll(parts[1], chan, 1),
                jnp.where(lane < half + chan, parts[2], pltpu.roll(parts[3], chan, 1)),
            ),
        )

    def start_patch(stage, buffer, value):
        buffer[me] = value
        copies_ = [
            remote(
                buffer.at[me],
                buffer.at[me],
                patch_send.at[stage, d - 1],
                patch_recv.at[stage, d - 1],
                lax.rem(me + d, patch_count),
                my_map,
            )
            for d in range(1, patch_count)
        ]
        sent.extend(copies_)
        return copies_

    def total_of(buffer, count, copies_):
        for copy in copies_:
            copy.wait_recv()
        result = buffer[0]
        for i in range(1, count):
            result = result + buffer[i]
        return result

    def start_map(stage, buffer, value):
        buffer[my_map] = value
        copies_ = [
            remote(
                buffer.at[my_map],
                buffer.at[my_map],
                map_send.at[stage, d - 1],
                map_recv.at[stage, d - 1],
                me,
                lax.rem(my_map + d, map_count),
            )
            for d in range(1, map_count)
        ]
        sent.extend(copies_)
        return copies_

    def pick(flag, yes, no):
        return jnp.where(flag, yes, no)

    def keep(flag, value):
        return jnp.where(flag, value, jnp.zeros_like(value))

    def left_part(w, b):
        return dot_nn(w[b], tiles[b, 1])

    def right_part(w, b):
        return dot_nn(w[b], tiles[b, 2])

    def send_adjoint(turn, w):
        p1 = {b: left_part(w, b) for b in low}
        p2 = {b: right_part(w, b) for b in high}
        last = nb - 1
        to_left[turn, 1] = (keep(near_left[0], p1[0]) + keep(~near_left[1], p1[1])).astype(BF16)
        to_left[turn, 0] = keep(~near_left[0], p1[0]).astype(BF16)
        to_right[turn, 0] = (keep(near_right[last], p2[last]) + keep(~near_right[last - 1], p2[last - 1])).astype(BF16)
        to_right[turn, 1] = keep(~near_right[last], p2[last]).astype(BF16)
        copies_ = [
            remote(to_left.at[turn], from_right.at[turn], adj_send.at[turn, 0], adj_recv.at[turn, 0], left, my_map),
            remote(to_right.at[turn], from_left.at[turn], adj_send.at[turn, 1], adj_recv.at[turn, 1], right, my_map),
        ]
        sent.extend(copies_)
        return copies_, p1, p2

    def local_adjoint(w, p1, p2):
        p1, p2 = dict(p1), dict(p2)
        for b in range(nb):
            if b not in p1:
                p1[b] = left_part(w, b)
            if b not in p2:
                p2[b] = right_part(w, b)
        for t in range(nb):
            value = dot_nn(w[t], tiles[t, 0])
            if t + 1 < nb:
                value = value + keep(near_left[t + 1], p1[t + 1])
            if t + 2 < nb:
                value = value + keep(~near_left[t + 2], p1[t + 2])
            if t >= 1:
                value = value + keep(near_right[t - 1], p2[t - 1])
            if t >= 2:
                value = value + keep(~near_right[t - 2], p2[t - 2])
            acc_y[t] = value

    def whole_adjoint(turn, t):
        value = acc_y[t]
        if t < reach:
            value = value + from_left[turn, t].astype(F32)
        if t >= nb - reach:
            value = value + from_right[turn, t - (nb - reach)].astype(F32)
        return value

    def turned(field, b, slot):
        if field is x_zero:
            turned_tiles[b, slot] = tiles[b, slot].T
        return turned_tiles[b, slot]

    def own_term(field, b):
        return dot_nn(field[reach + b], turned(field, b, 0))

    def left_term(field, b):
        return dot_nn(pick(near_left[b], field[reach + b - 1], field[reach + b - 2]), turned(field, b, 1))

    def right_term(field, b):
        return dot_nn(pick(near_right[b], field[reach + b + 1], field[reach + b + 2]), turned(field, b, 2))

    def inner_forward(field, b):
        value = own_term(field, b)
        if b >= reach:
            value = value + left_term(field, b)
        if b < nb - reach:
            value = value + right_term(field, b)
        return value

    def rest_forward(field, b):
        return left_term(field, b) if b < reach else right_term(field, b)

    pl.semaphore_wait(barrier, patch_count + map_count - 2)
    halo = send_maps()
    load_c.wait()
    near_left = [lax.rem(me * nb + b - cols[1, b] + total, total) == 1 for b in range(nb)]
    near_right = [lax.rem(cols[2, b] - me * nb - b + total, total) == 1 for b in range(nb)]
    for b in edges:
        loads_y[b].wait()
        loads_t[b].wait()
    adj, p1, p2 = send_adjoint(0, y_zero)
    for b in middle:
        loads_y[b].wait()
        loads_t[b].wait()
    for b in range(nb):
        loads_x[b].wait()
    for b in edges:
        acc_x[b] = inner_forward(x_zero, b)
    local_adjoint(y_zero, p1, p2)
    for copy in halo:
        copy.wait_recv()
    for b in edges:
        x_one[reach + b] = (acc_x[b] + rest_forward(x_zero, b)).astype(BF16)
    halo = send_x_one()
    for b in middle:
        x_one[reach + b] = inner_forward(x_zero, b).astype(BF16)

    product = None
    for b in range(nb):
        rows = jnp.concatenate([x_zero[reach + b], x_one[reach + b]], axis=0)
        term = dot_nt(rows, jnp.concatenate([y_zero[b], y_zero[b]], axis=0))
        product = term if product is None else product + term
    zeroth, first_order = fold(product[:half]), fold(product[half:])
    mid = chan // 2
    early = start_patch(0, early_patch, lanes([zeroth[:mid], zeroth[mid:], first_order[:mid], first_order[mid:]]))

    for copy in adj:
        copy.wait_recv()
    product = None
    for b in range(nb):
        y_one[b] = whole_adjoint(0, b).astype(BF16)
        term = dot_nt(x_one[reach + b], jnp.concatenate([y_one[b], y_one[b]], axis=0))
        product = term if product is None else product + term
    second = fold(product)
    quarter = chan // 4
    late = start_patch(1, late_patch, lanes([second[i * quarter : (i + 1) * quarter] for i in range(4)]))

    adj, p1, p2 = send_adjoint(1, y_one)
    early = start_map(0, early_map, total_of(early_patch, patch_count, early))
    for b in edges:
        acc_x[b] = inner_forward(x_one, b)

    def write_output(b, applied):
        first = x_zero[reach + b]
        x_two = (2.0 * applied - first.astype(F32)).astype(BF16)
        terms = jnp.concatenate([first, x_one[reach + b], x_two], axis=0)
        out[:, b * bs : (b + 1) * bs] = dot_nn(mix_out[:, : terms.shape[0]], terms).astype(BF16)

    def write_grad(b):
        first = y_zero[b]
        y_two = 2.0 * whole_adjoint(1, b) - first.astype(F32)
        coarse = y_two.astype(BF16)
        fine = (y_two - coarse.astype(F32)).astype(BF16)
        terms = jnp.concatenate([first, y_one[b], coarse, fine], axis=0)
        grad[:, b * bs : (b + 1) * bs] = dot_nn(mix_in[...], terms).astype(BF16)

    load_f.wait()
    mix_in[...], mix_out[...] = mixing(filters, copies)
    late = start_map(1, late_map, total_of(late_patch, patch_count, late))
    local_adjoint(y_one, p1, p2)
    for b in middle:
        write_output(b, inner_forward(x_one, b))
        write_grad(b)
    for copy in halo:
        copy.wait_recv()
    for b in edges:
        write_output(b, acc_x[b] + rest_forward(x_one, b))
    for copy in adj:
        copy.wait_recv()
    for b in edges:
        write_grad(b)
    whole = total_of(early_map, map_count, early) * scale
    shifted = [pltpu.roll(whole, width - i * chan, 1)[:, :chan] if i else whole[:, :chan] for i in range(4)]
    filter_grad[0, :mid], filter_grad[0, mid:] = shifted[0], shifted[1]
    filter_grad[1, :mid], filter_grad[1, mid:] = shifted[2], shifted[3]
    whole = total_of(late_map, map_count, late) * scale
    for i in range(4):
        lines = slice(i * quarter, (i + 1) * quarter)
        part = pltpu.roll(whole, width - i * chan, 1)[:, :chan] if i else whole[:, :chan]
        filter_grad[2, lines] = 2.0 * part - filter_grad[0, lines]
    for copy in sent:
        copy.wait_send()


def write(out, grad, filter_grad, out_hbm, grad_hbm, filter_grad_hbm, sems):
    copies = [
        pltpu.make_async_copy(out, out_hbm, sems.at[0]),
        pltpu.make_async_copy(grad, grad_hbm, sems.at[1]),
        pltpu.make_async_copy(filter_grad, filter_grad_hbm, sems.at[2]),
    ]
    for copy in copies:
        copy.start()
    for copy in copies:
        copy.wait()


def per_device(patch_count, map_count, maps, cotangent, tiles, columns, filters):
    copies, chan, pix = maps.shape
    nb, slots, bs, _ = tiles.shape
    rows = copies * chan
    order = filters.shape[0]
    scale = 1.0 / math.sqrt(copies * map_count * pix * patch_count)
    hbm = pl.BlockSpec(memory_space=pltpu.HBM)
    vmem = pl.BlockSpec(memory_space=pltpu.VMEM)
    dma = pltpu.SemaphoreType.DMA
    field = pltpu.VMEM((nb + 2 * REACH, rows, bs), BF16)
    own = pltpu.VMEM((nb, rows, bs), BF16)
    wide = pltpu.VMEM((nb, rows, bs), F32)
    rim = pltpu.VMEM((2, REACH, rows, bs), BF16)
    pin = lambda x: pltpu.with_memory_space_constraint(x, pltpu.HBM)
    results = (
        jax.ShapeDtypeStruct((rows, pix), BF16),
        jax.ShapeDtypeStruct((rows, pix), BF16),
        jax.ShapeDtypeStruct((order, chan, chan), F32),
    )
    held = pl.pallas_call(
        functools.partial(kernel, patch_count, map_count, copies, scale),
        out_shape=results,
        in_specs=[hbm, hbm, hbm, hbm, hbm],
        out_specs=(vmem, vmem, vmem),
        scratch_shapes=[
            pltpu.SMEM((slots, nb), jnp.int32),
            pltpu.VMEM((order, chan, chan), BF16),
            pltpu.VMEM((nb, slots, bs, bs), BF16),
            pltpu.VMEM((nb, slots, bs, bs), BF16),
            field,
            field,
            own,
            own,
            wide,
            wide,
            rim,
            rim,
            rim,
            rim,
            pltpu.VMEM((patch_count, chan // 2, 2 * rows), F32),
            pltpu.VMEM((map_count, chan // 2, 2 * rows), F32),
            pltpu.VMEM((patch_count, chan // 4, 2 * rows), F32),
            pltpu.VMEM((map_count, chan // 4, 2 * rows), F32),
            pltpu.VMEM((rows, 4 * rows), BF16),
            pltpu.VMEM((rows, 4 * rows), BF16),
            dma,
            dma,
            dma((nb,)),
            dma((nb,)),
            dma((nb,)),
            dma((2, 2, REACH)),
            dma((2, 2, REACH)),
            dma((2, 2)),
            dma((2, 2)),
            dma((2, patch_count - 1)),
            dma((2, patch_count - 1)),
            dma((2, map_count - 1)),
            dma((2, map_count - 1)),
        ],
        compiler_params=pltpu.CompilerParams(
            collective_id=0, has_side_effects=True, vmem_limit_bytes=40 * 1024 * 1024
        ),
    )(
        pin(maps.reshape(rows, pix)), pin(cotangent.reshape(rows, pix)), pin(tiles), pin(columns.T), pin(filters)
    )
    out, grad, filter_grad = pl.pallas_call(
        write,
        out_shape=results,
        in_specs=[vmem] * 3,
        out_specs=(hbm,) * 3,
        scratch_shapes=[dma((3,))],
        compiler_params=pltpu.CompilerParams(vmem_limit_bytes=4 * 1024 * 1024),
    )(*held)
    return out.reshape(copies, chan, pix), grad.reshape(copies, chan, pix), filter_grad


def solution(mesh):
    field = P("map", None, "patch")
    return jax.shard_map(
        functools.partial(per_device, mesh.shape["patch"], mesh.shape["map"]),
        mesh=mesh,
        in_specs=(field, field, P("patch", None, None, None), P("patch", None), P()),
        out_specs=(field, field, P()),
        check_vma=False,
    )
```

```python
import functools
import math

import jax
import jax.numpy as jnp
from jax import lax
from jax.experimental import pallas as pl
from jax.experimental.pallas import tpu as pltpu
from jax.sharding import PartitionSpec as P

REACH = 2
MESH = pl.DeviceIdType.MESH
F32 = jnp.float32
BF16 = jnp.bfloat16


def dot_nn(a, b):
    return lax.dot_general(a, b, (((1,), (0,)), ((), ())), preferred_element_type=F32)


def dot_nt(a, b):
    return lax.dot_general(a, b, (((1,), (1,)), ((), ())), preferred_element_type=F32)


def mixing(filters, copies):
    order, chan = filters.shape[0], filters.shape[1]
    zero = jnp.zeros((chan, chan), F32)
    adjoint, output = [], []
    for m in range(copies):
        adjoint.append([])
        output.append([])
        for k in list(range(order)) + [order - 1]:
            term = filters[k].astype(F32)
            for n in range(copies):
                adjoint[m].append(term if n == m else zero)
                output[m].append(term.T if n == m else zero)
    join = lambda rows: jnp.concatenate([jnp.concatenate(r, axis=1) for r in rows], axis=0).astype(BF16)
    return join(adjoint), join(output)


def kernel(
    patch_count,
    map_count,
    copies,
    scale,
    maps,
    cot,
    tiles_hbm,
    cols_hbm,
    filters_hbm,
    out,
    grad,
    filter_grad,
    cols,
    filters,
    tiles,
    turned_tiles,
    x_zero,
    x_one,
    y_zero,
    y_one,
    acc_x,
    acc_y,
    to_left,
    to_right,
    from_left,
    from_right,
    early_patch,
    early_map,
    late_patch,
    late_map,
    mix_out,
    mix_in,
    load_cols,
    load_filters,
    load_tile,
    load_x,
    load_y,
    halo_send,
    halo_recv,
    adj_send,
    adj_recv,
    patch_send,
    patch_recv,
    map_send,
    map_recv,
):
    nb, _, bs, _ = tiles.shape
    reach = REACH
    me, my_map = lax.axis_index("patch"), lax.axis_index("map")
    left = lax.rem(me + patch_count - 1, patch_count)
    right = lax.rem(me + 1, patch_count)
    total = patch_count * nb
    low = list(range(reach))
    high = list(range(nb - reach, nb))
    middle = list(range(reach, nb - reach))
    edges = [b for pair in zip(low, reversed(high)) for b in pair]
    order = edges + middle

    barrier = pltpu.get_barrier_semaphore()
    for d in range(1, patch_count):
        pl.semaphore_signal(barrier, inc=1, device_id=(lax.rem(me + d, patch_count), my_map), device_id_type=MESH)
    for d in range(1, map_count):
        pl.semaphore_signal(barrier, inc=1, device_id=(me, lax.rem(my_map + d, map_count)), device_id_type=MESH)

    loads_y = [pltpu.make_async_copy(cot.at[:, pl.ds(b * bs, bs)], y_zero.at[b], load_y.at[b]) for b in range(nb)]
    loads_x = [pltpu.make_async_copy(maps.at[:, pl.ds(b * bs, bs)], x_zero.at[reach + b], load_x.at[b]) for b in range(nb)]
    loads_t = [pltpu.make_async_copy(tiles_hbm.at[b], tiles.at[b], load_tile.at[b]) for b in range(nb)]
    for b in order:
        loads_x[b].start()
    load_f = pltpu.make_async_copy(filters_hbm, filters, load_filters)
    load_f.start()
    load_c = pltpu.make_async_copy(cols_hbm, cols, load_cols)
    load_c.start()
    for b in order:
        loads_y[b].start()
        loads_t[b].start()
    def remote(src, dst, send_sem, recv_sem, patch, map_index):
        copy = pltpu.make_async_remote_copy(
            src_ref=src,
            dst_ref=dst,
            send_sem=send_sem,
            recv_sem=recv_sem,
            device_id=(patch, map_index),
            device_id_type=MESH,
        )
        copy.start()
        return copy

    sent = []

    def send_halo(turn, field):
        copies_ = [
            remote(
                field.at[pl.ds(reach, reach)],
                field.at[pl.ds(reach + nb, reach)],
                halo_send.at[turn, 0],
                halo_recv.at[turn, 0],
                left,
                my_map,
            ),
            remote(
                field.at[pl.ds(nb, reach)],
                field.at[pl.ds(0, reach)],
                halo_send.at[turn, 1],
                halo_recv.at[turn, 1],
                right,
                my_map,
            ),
        ]
        sent.extend(copies_)
        return copies_

    chan = filters.shape[1]
    half = copies * chan
    width = 2 * half

    def fold(value):
        result = value[:chan]
        for m in range(1, copies):
            result = result + pltpu.roll(value[m * chan : (m + 1) * chan], width - m * chan, 1)
        return result

    def lanes(parts):
        lane = lax.broadcasted_iota(jnp.int32, parts[0].shape, 1)
        return jnp.where(
            lane < chan,
            parts[0],
            jnp.where(
                lane < half,
                pltpu.roll(parts[1], chan, 1),
                jnp.where(lane < half + chan, parts[2], pltpu.roll(parts[3], chan, 1)),
            ),
        )

    def start_patch(stage, buffer, value):
        buffer[me] = value
        copies_ = [
            remote(
                buffer.at[me],
                buffer.at[me],
                patch_send.at[stage, d - 1],
                patch_recv.at[stage, d - 1],
                lax.rem(me + d, patch_count),
                my_map,
            )
            for d in range(1, patch_count)
        ]
        sent.extend(copies_)
        return copies_

    def total_of(buffer, count, copies_):
        for copy in copies_:
            copy.wait_recv()
        result = buffer[0]
        for i in range(1, count):
            result = result + buffer[i]
        return result

    def start_map(stage, buffer, value):
        buffer[my_map] = value
        copies_ = [
            remote(
                buffer.at[my_map],
                buffer.at[my_map],
                map_send.at[stage, d - 1],
                map_recv.at[stage, d - 1],
                me,
                lax.rem(my_map + d, map_count),
            )
            for d in range(1, map_count)
        ]
        sent.extend(copies_)
        return copies_

    def pick(flag, yes, no):
        return jnp.where(flag, yes, no)

    def keep(flag, value):
        return jnp.where(flag, value, jnp.zeros_like(value))

    def left_part(w, b):
        return dot_nn(w[b], tiles[b, 1])

    def right_part(w, b):
        return dot_nn(w[b], tiles[b, 2])

    def send_adjoint(turn, w):
        p1 = {b: left_part(w, b) for b in low}
        p2 = {b: right_part(w, b) for b in high}
        last = nb - 1
        to_left[turn, 1] = (keep(near_left[0], p1[0]) + keep(~near_left[1], p1[1])).astype(BF16)
        to_left[turn, 0] = keep(~near_left[0], p1[0]).astype(BF16)
        to_right[turn, 0] = (keep(near_right[last], p2[last]) + keep(~near_right[last - 1], p2[last - 1])).astype(BF16)
        to_right[turn, 1] = keep(~near_right[last], p2[last]).astype(BF16)
        copies_ = [
            remote(to_left.at[turn], from_right.at[turn], adj_send.at[turn, 0], adj_recv.at[turn, 0], left, my_map),
            remote(to_right.at[turn], from_left.at[turn], adj_send.at[turn, 1], adj_recv.at[turn, 1], right, my_map),
        ]
        sent.extend(copies_)
        return copies_, p1, p2

    def local_adjoint(w, p1, p2):
        p1, p2 = dict(p1), dict(p2)
        for b in range(nb):
            if b not in p1:
                p1[b] = left_part(w, b)
            if b not in p2:
                p2[b] = right_part(w, b)
        for t in range(nb):
            value = dot_nn(w[t], tiles[t, 0])
            if t + 1 < nb:
                value = value + keep(near_left[t + 1], p1[t + 1])
            if t + 2 < nb:
                value = value + keep(~near_left[t + 2], p1[t + 2])
            if t >= 1:
                value = value + keep(near_right[t - 1], p2[t - 1])
            if t >= 2:
                value = value + keep(~near_right[t - 2], p2[t - 2])
            acc_y[t] = value

    def whole_adjoint(turn, t):
        value = acc_y[t]
        if t < reach:
            value = value + from_left[turn, t].astype(F32)
        if t >= nb - reach:
            value = value + from_right[turn, t - (nb - reach)].astype(F32)
        return value

    def turned(field, b, slot):
        if field is x_zero:
            turned_tiles[b, slot] = tiles[b, slot].T
        return turned_tiles[b, slot]

    def own_term(field, b):
        return dot_nn(field[reach + b], turned(field, b, 0))

    def left_term(field, b):
        return dot_nn(pick(near_left[b], field[reach + b - 1], field[reach + b - 2]), turned(field, b, 1))

    def right_term(field, b):
        return dot_nn(pick(near_right[b], field[reach + b + 1], field[reach + b + 2]), turned(field, b, 2))

    def inner_forward(field, b):
        value = own_term(field, b)
        if b >= reach:
            value = value + left_term(field, b)
        if b < nb - reach:
            value = value + right_term(field, b)
        return value

    def rest_forward(field, b):
        return left_term(field, b) if b < reach else right_term(field, b)

    pl.semaphore_wait(barrier, patch_count + map_count - 2)
    for b in edges:
        loads_x[b].wait()
    halo = send_halo(0, x_zero)
    load_c.wait()
    near_left = [lax.rem(me * nb + b - cols[1, b] + total, total) == 1 for b in range(nb)]
    near_right = [lax.rem(cols[2, b] - me * nb - b + total, total) == 1 for b in range(nb)]
    for b in edges:
        loads_y[b].wait()
        loads_t[b].wait()
    adj, p1, p2 = send_adjoint(0, y_zero)
    for b in middle:
        loads_y[b].wait()
        loads_t[b].wait()
    for b in middle:
        loads_x[b].wait()
    for b in edges:
        acc_x[b] = inner_forward(x_zero, b)
    local_adjoint(y_zero, p1, p2)
    for copy in halo:
        copy.wait_recv()
    for b in edges:
        x_one[reach + b] = (acc_x[b] + rest_forward(x_zero, b)).astype(BF16)
    halo = send_halo(1, x_one)
    for b in middle:
        x_one[reach + b] = inner_forward(x_zero, b).astype(BF16)

    product = None
    for b in range(nb):
        rows = jnp.concatenate([x_zero[reach + b], x_one[reach + b]], axis=0)
        term = dot_nt(rows, jnp.concatenate([y_zero[b], y_zero[b]], axis=0))
        product = term if product is None else product + term
    zeroth, first_order = fold(product[:half]), fold(product[half:])
    mid = chan // 2
    early = start_patch(0, early_patch, lanes([zeroth[:mid], zeroth[mid:], first_order[:mid], first_order[mid:]]))

    for copy in adj:
        copy.wait_recv()
    product = None
    for b in range(nb):
        y_one[b] = whole_adjoint(0, b).astype(BF16)
        term = dot_nt(x_one[reach + b], jnp.concatenate([y_one[b], y_one[b]], axis=0))
        product = term if product is None else product + term
    second = fold(product)
    quarter = chan // 4
    late = start_patch(1, late_patch, lanes([second[i * quarter : (i + 1) * quarter] for i in range(4)]))

    adj, p1, p2 = send_adjoint(1, y_one)
    early = start_map(0, early_map, total_of(early_patch, patch_count, early))
    for b in edges:
        acc_x[b] = inner_forward(x_one, b)

    def write_output(b, applied):
        first = x_zero[reach + b]
        x_two = (2.0 * applied - first.astype(F32)).astype(BF16)
        terms = jnp.concatenate([first, x_one[reach + b], x_two], axis=0)
        out[:, b * bs : (b + 1) * bs] = dot_nn(mix_out[:, : terms.shape[0]], terms).astype(BF16)

    def write_grad(b):
        first = y_zero[b]
        y_two = 2.0 * whole_adjoint(1, b) - first.astype(F32)
        coarse = y_two.astype(BF16)
        fine = (y_two - coarse.astype(F32)).astype(BF16)
        terms = jnp.concatenate([first, y_one[b], coarse, fine], axis=0)
        grad[:, b * bs : (b + 1) * bs] = dot_nn(mix_in[...], terms).astype(BF16)

    load_f.wait()
    mix_in[...], mix_out[...] = mixing(filters, copies)
    late = start_map(1, late_map, total_of(late_patch, patch_count, late))
    local_adjoint(y_one, p1, p2)
    for b in middle:
        write_output(b, inner_forward(x_one, b))
        write_grad(b)
    for copy in halo:
        copy.wait_recv()
    for b in edges:
        write_output(b, acc_x[b] + rest_forward(x_one, b))
    for copy in adj:
        copy.wait_recv()
    for b in edges:
        write_grad(b)
    whole = total_of(early_map, map_count, early) * scale
    shifted = [pltpu.roll(whole, width - i * chan, 1)[:, :chan] if i else whole[:, :chan] for i in range(4)]
    filter_grad[0, :mid], filter_grad[0, mid:] = shifted[0], shifted[1]
    filter_grad[1, :mid], filter_grad[1, mid:] = shifted[2], shifted[3]
    whole = total_of(late_map, map_count, late) * scale
    for i in range(4):
        lines = slice(i * quarter, (i + 1) * quarter)
        part = pltpu.roll(whole, width - i * chan, 1)[:, :chan] if i else whole[:, :chan]
        filter_grad[2, lines] = 2.0 * part - filter_grad[0, lines]
    for copy in sent:
        copy.wait_send()


def write(out, grad, filter_grad, out_hbm, grad_hbm, filter_grad_hbm, sems):
    copies = [
        pltpu.make_async_copy(out, out_hbm, sems.at[0]),
        pltpu.make_async_copy(grad, grad_hbm, sems.at[1]),
        pltpu.make_async_copy(filter_grad, filter_grad_hbm, sems.at[2]),
    ]
    for copy in copies:
        copy.start()
    for copy in copies:
        copy.wait()


def per_device(patch_count, map_count, maps, cotangent, tiles, columns, filters):
    copies, chan, pix = maps.shape
    nb, slots, bs, _ = tiles.shape
    rows = copies * chan
    order = filters.shape[0]
    scale = 1.0 / math.sqrt(copies * map_count * pix * patch_count)
    hbm = pl.BlockSpec(memory_space=pltpu.HBM)
    vmem = pl.BlockSpec(memory_space=pltpu.VMEM)
    dma = pltpu.SemaphoreType.DMA
    field = pltpu.VMEM((nb + 2 * REACH, rows, bs), BF16)
    own = pltpu.VMEM((nb, rows, bs), BF16)
    wide = pltpu.VMEM((nb, rows, bs), F32)
    rim = pltpu.VMEM((2, REACH, rows, bs), BF16)
    pin = lambda x: pltpu.with_memory_space_constraint(x, pltpu.HBM)
    results = (
        jax.ShapeDtypeStruct((rows, pix), BF16),
        jax.ShapeDtypeStruct((rows, pix), BF16),
        jax.ShapeDtypeStruct((order, chan, chan), F32),
    )
    held = pl.pallas_call(
        functools.partial(kernel, patch_count, map_count, copies, scale),
        out_shape=results,
        in_specs=[hbm, hbm, hbm, hbm, hbm],
        out_specs=(vmem, vmem, vmem),
        scratch_shapes=[
            pltpu.SMEM((slots, nb), jnp.int32),
            pltpu.VMEM((order, chan, chan), BF16),
            pltpu.VMEM((nb, slots, bs, bs), BF16),
            pltpu.VMEM((nb, slots, bs, bs), BF16),
            field,
            field,
            own,
            own,
            wide,
            wide,
            rim,
            rim,
            rim,
            rim,
            pltpu.VMEM((patch_count, chan // 2, 2 * rows), F32),
            pltpu.VMEM((map_count, chan // 2, 2 * rows), F32),
            pltpu.VMEM((patch_count, chan // 4, 2 * rows), F32),
            pltpu.VMEM((map_count, chan // 4, 2 * rows), F32),
            pltpu.VMEM((rows, 4 * rows), BF16),
            pltpu.VMEM((rows, 4 * rows), BF16),
            dma,
            dma,
            dma((nb,)),
            dma((nb,)),
            dma((nb,)),
            dma((2, 2)),
            dma((2, 2)),
            dma((2, 2)),
            dma((2, 2)),
            dma((2, patch_count - 1)),
            dma((2, patch_count - 1)),
            dma((2, map_count - 1)),
            dma((2, map_count - 1)),
        ],
        compiler_params=pltpu.CompilerParams(
            collective_id=0, has_side_effects=True, vmem_limit_bytes=40 * 1024 * 1024
        ),
    )(
        pin(maps.reshape(rows, pix)), pin(cotangent.reshape(rows, pix)), pin(tiles), pin(columns.T), pin(filters)
    )
    out, grad, filter_grad = pl.pallas_call(
        write,
        out_shape=results,
        in_specs=[vmem] * 3,
        out_specs=(hbm,) * 3,
        scratch_shapes=[dma((3,))],
        compiler_params=pltpu.CompilerParams(vmem_limit_bytes=4 * 1024 * 1024),
    )(*held)
    return out.reshape(copies, chan, pix), grad.reshape(copies, chan, pix), filter_grad


def solution(mesh):
    field = P("map", None, "patch")
    return jax.shard_map(
        functools.partial(per_device, mesh.shape["patch"], mesh.shape["map"]),
        mesh=mesh,
        in_specs=(field, field, P("patch", None, None, None), P("patch", None), P()),
        out_specs=(field, field, P()),
        check_vma=False,
    )
```

```python
import functools
import math

import jax
import jax.numpy as jnp
from jax import lax
from jax.experimental import pallas as pl
from jax.experimental.pallas import tpu as pltpu
from jax.sharding import PartitionSpec as P

REACH = 2
MESH = pl.DeviceIdType.MESH
F32 = jnp.float32
BF16 = jnp.bfloat16


def dot_nn(a, b):
    return lax.dot_general(a, b, (((1,), (0,)), ((), ())), preferred_element_type=F32)


def dot_nt(a, b):
    return lax.dot_general(a, b, (((1,), (1,)), ((), ())), preferred_element_type=F32)


def mixing(filters, copies):
    order, chan = filters.shape[0], filters.shape[1]
    zero = jnp.zeros((chan, chan), F32)
    adjoint, output = [], []
    for m in range(copies):
        adjoint.append([])
        output.append([])
        for k in list(range(order)) + [order - 1]:
            term = filters[k].astype(F32)
            for n in range(copies):
                adjoint[m].append(term if n == m else zero)
                output[m].append(term.T if n == m else zero)
    join = lambda rows: jnp.concatenate([jnp.concatenate(r, axis=1) for r in rows], axis=0).astype(BF16)
    return join(adjoint), join(output)


def kernel(
    patch_count,
    map_count,
    copies,
    scale,
    maps,
    cot,
    tiles_hbm,
    cols_hbm,
    filters_hbm,
    out,
    grad,
    filter_grad,
    cols,
    filters,
    tiles,
    turned_tiles,
    x_zero,
    x_one,
    y_zero,
    y_one,
    acc_x,
    acc_y,
    to_left,
    to_right,
    from_left,
    from_right,
    early_patch,
    early_map,
    late_patch,
    late_map,
    mix_out,
    mix_in,
    load_cols,
    load_filters,
    load_tile,
    load_x,
    load_y,
    halo_send,
    halo_recv,
    adj_send,
    adj_recv,
    patch_send,
    patch_recv,
    map_send,
    map_recv,
):
    nb, _, bs, _ = tiles.shape
    reach = REACH
    me, my_map = lax.axis_index("patch"), lax.axis_index("map")
    left = lax.rem(me + patch_count - 1, patch_count)
    right = lax.rem(me + 1, patch_count)
    total = patch_count * nb
    low = list(range(reach))
    high = list(range(nb - reach, nb))
    middle = list(range(reach, nb - reach))
    edges = [b for pair in zip(low, reversed(high)) for b in pair]
    order = edges + middle

    barrier = pltpu.get_barrier_semaphore()
    for d in range(1, patch_count):
        pl.semaphore_signal(barrier, inc=1, device_id=(lax.rem(me + d, patch_count), my_map), device_id_type=MESH)
    for d in range(1, map_count):
        pl.semaphore_signal(barrier, inc=1, device_id=(me, lax.rem(my_map + d, map_count)), device_id_type=MESH)

    loads_y = [pltpu.make_async_copy(cot.at[:, pl.ds(b * bs, bs)], y_zero.at[b], load_y.at[b]) for b in range(nb)]
    loads_x = [pltpu.make_async_copy(maps.at[:, pl.ds(b * bs, bs)], x_zero.at[reach + b], load_x.at[b]) for b in range(nb)]
    loads_t = [pltpu.make_async_copy(tiles_hbm.at[b], tiles.at[b], load_tile.at[b]) for b in range(nb)]
    for b in order:
        loads_x[b].start()
    load_f = pltpu.make_async_copy(filters_hbm, filters, load_filters)
    load_f.start()
    load_c = pltpu.make_async_copy(cols_hbm, cols, load_cols)
    load_c.start()
    for b in order:
        loads_y[b].start()
        loads_t[b].start()
    def remote(src, dst, send_sem, recv_sem, patch, map_index):
        copy = pltpu.make_async_remote_copy(
            src_ref=src,
            dst_ref=dst,
            send_sem=send_sem,
            recv_sem=recv_sem,
            device_id=(patch, map_index),
            device_id_type=MESH,
        )
        copy.start()
        return copy

    sent = []

    def send_halo(turn, field):
        copies_ = [
            remote(
                field.at[pl.ds(reach, reach)],
                field.at[pl.ds(reach + nb, reach)],
                halo_send.at[turn, 0],
                halo_recv.at[turn, 0],
                left,
                my_map,
            ),
            remote(
                field.at[pl.ds(nb, reach)],
                field.at[pl.ds(0, reach)],
                halo_send.at[turn, 1],
                halo_recv.at[turn, 1],
                right,
                my_map,
            ),
        ]
        sent.extend(copies_)
        return copies_

    chan = filters.shape[1]
    half = copies * chan
    width = 2 * half

    def fold(value):
        result = value[:chan]
        for m in range(1, copies):
            result = result + pltpu.roll(value[m * chan : (m + 1) * chan], width - m * chan, 1)
        return result

    def lanes(parts):
        lane = lax.broadcasted_iota(jnp.int32, parts[0].shape, 1)
        return jnp.where(
            lane < chan,
            parts[0],
            jnp.where(
                lane < half,
                pltpu.roll(parts[1], chan, 1),
                jnp.where(lane < half + chan, parts[2], pltpu.roll(parts[3], chan, 1)),
            ),
        )

    def start_patch(stage, buffer, value):
        buffer[me] = value
        copies_ = [
            remote(
                buffer.at[me],
                buffer.at[me],
                patch_send.at[stage, d - 1],
                patch_recv.at[stage, d - 1],
                lax.rem(me + d, patch_count),
                my_map,
            )
            for d in range(1, patch_count)
        ]
        sent.extend(copies_)
        return copies_

    def total_of(buffer, count, copies_):
        for copy in copies_:
            copy.wait_recv()
        result = buffer[0]
        for i in range(1, count):
            result = result + buffer[i]
        return result

    def start_map(stage, buffer, value):
        buffer[my_map] = value
        copies_ = [
            remote(
                buffer.at[my_map],
                buffer.at[my_map],
                map_send.at[stage, d - 1],
                map_recv.at[stage, d - 1],
                me,
                lax.rem(my_map + d, map_count),
            )
            for d in range(1, map_count)
        ]
        sent.extend(copies_)
        return copies_

    def pick(flag, yes, no):
        return jnp.where(flag, yes, no)

    def keep(flag, value):
        return jnp.where(flag, value, jnp.zeros_like(value))

    def left_part(w, b):
        return dot_nn(w[b], tiles[b, 1])

    def right_part(w, b):
        return dot_nn(w[b], tiles[b, 2])

    def send_adjoint(turn, w):
        p1 = {b: left_part(w, b) for b in low}
        p2 = {b: right_part(w, b) for b in high}
        last = nb - 1
        to_left[turn, 1] = (keep(near_left[0], p1[0]) + keep(~near_left[1], p1[1])).astype(BF16)
        to_left[turn, 0] = keep(~near_left[0], p1[0]).astype(BF16)
        to_right[turn, 0] = (keep(near_right[last], p2[last]) + keep(~near_right[last - 1], p2[last - 1])).astype(BF16)
        to_right[turn, 1] = keep(~near_right[last], p2[last]).astype(BF16)
        copies_ = [
            remote(to_left.at[turn], from_right.at[turn], adj_send.at[turn, 0], adj_recv.at[turn, 0], left, my_map),
            remote(to_right.at[turn], from_left.at[turn], adj_send.at[turn, 1], adj_recv.at[turn, 1], right, my_map),
        ]
        sent.extend(copies_)
        return copies_, p1, p2

    def local_adjoint(w, p1, p2):
        p1, p2 = dict(p1), dict(p2)
        for b in range(nb):
            if b not in p1:
                p1[b] = left_part(w, b)
            if b not in p2:
                p2[b] = right_part(w, b)
        for t in range(nb):
            value = dot_nn(w[t], tiles[t, 0])
            if t + 1 < nb:
                value = value + keep(near_left[t + 1], p1[t + 1])
            if t + 2 < nb:
                value = value + keep(~near_left[t + 2], p1[t + 2])
            if t >= 1:
                value = value + keep(near_right[t - 1], p2[t - 1])
            if t >= 2:
                value = value + keep(~near_right[t - 2], p2[t - 2])
            acc_y[t] = value

    def whole_adjoint(turn, t):
        value = acc_y[t]
        if t < reach:
            value = value + from_left[turn, t].astype(F32)
        if t >= nb - reach:
            value = value + from_right[turn, t - (nb - reach)].astype(F32)
        return value

    def turned(field, b, slot):
        if field is x_zero:
            turned_tiles[b, slot] = tiles[b, slot].T
        return turned_tiles[b, slot]

    def own_term(field, b):
        return dot_nn(field[reach + b], turned(field, b, 0))

    def left_term(field, b):
        return dot_nn(pick(near_left[b], field[reach + b - 1], field[reach + b - 2]), turned(field, b, 1))

    def right_term(field, b):
        return dot_nn(pick(near_right[b], field[reach + b + 1], field[reach + b + 2]), turned(field, b, 2))

    def inner_forward(field, b):
        value = own_term(field, b)
        if b >= reach:
            value = value + left_term(field, b)
        if b < nb - reach:
            value = value + right_term(field, b)
        return value

    def rest_forward(field, b):
        return left_term(field, b) if b < reach else right_term(field, b)

    pl.semaphore_wait(barrier, patch_count + map_count - 2)
    for b in edges:
        loads_x[b].wait()
    halo = send_halo(0, x_zero)
    load_c.wait()
    near_left = [lax.rem(me * nb + b - cols[1, b] + total, total) == 1 for b in range(nb)]
    near_right = [lax.rem(cols[2, b] - me * nb - b + total, total) == 1 for b in range(nb)]
    for b in edges:
        loads_y[b].wait()
        loads_t[b].wait()
    adj, p1, p2 = send_adjoint(0, y_zero)
    for b in middle:
        loads_y[b].wait()
        loads_t[b].wait()
    for b in middle:
        loads_x[b].wait()
    for b in edges:
        acc_x[b] = inner_forward(x_zero, b)
    local_adjoint(y_zero, p1, p2)
    for copy in halo:
        copy.wait_recv()
    for b in edges:
        x_one[reach + b] = (acc_x[b] + rest_forward(x_zero, b)).astype(BF16)
    halo = send_halo(1, x_one)
    for b in middle:
        x_one[reach + b] = inner_forward(x_zero, b).astype(BF16)

    product = None
    for b in range(nb):
        rows = jnp.concatenate([x_zero[reach + b], x_one[reach + b]], axis=0)
        term = dot_nt(rows, jnp.concatenate([y_zero[b], y_zero[b]], axis=0))
        product = term if product is None else product + term
    zeroth, first_order = fold(product[:half]), fold(product[half:])
    mid = chan // 2
    early = start_patch(0, early_patch, lanes([zeroth[:mid], zeroth[mid:], first_order[:mid], first_order[mid:]]))

    for copy in adj:
        copy.wait_recv()
    product = None
    for b in range(nb):
        y_one[b] = whole_adjoint(0, b).astype(BF16)
        term = dot_nt(x_one[reach + b], jnp.concatenate([y_one[b], y_one[b]], axis=0))
        product = term if product is None else product + term
    second = fold(product)
    quarter = chan // 4
    late = start_patch(1, late_patch, lanes([second[i * quarter : (i + 1) * quarter] for i in range(4)]))

    adj, p1, p2 = send_adjoint(1, y_one)
    early = start_map(0, early_map, total_of(early_patch, patch_count, early))
    for b in edges:
        acc_x[b] = inner_forward(x_one, b)

    def write_output(b, applied):
        first = x_zero[reach + b]
        x_two = (2.0 * applied - first.astype(F32)).astype(BF16)
        terms = jnp.concatenate([first, x_one[reach + b], x_two], axis=0)
        out[:, b * bs : (b + 1) * bs] = dot_nn(mix_out[:, : terms.shape[0]], terms).astype(BF16)

    def write_grad(b):
        first = y_zero[b]
        y_two = 2.0 * whole_adjoint(1, b) - first.astype(F32)
        coarse = y_two.astype(BF16)
        fine = (y_two - coarse.astype(F32)).astype(BF16)
        terms = jnp.concatenate([first, y_one[b], coarse, fine], axis=0)
        grad[:, b * bs : (b + 1) * bs] = dot_nn(mix_in[...], terms).astype(BF16)

    load_f.wait()
    mix_in[...], mix_out[...] = mixing(filters, copies)
    late = start_map(1, late_map, total_of(late_patch, patch_count, late))
    local_adjoint(y_one, p1, p2)
    for b in middle:
        write_output(b, inner_forward(x_one, b))
        write_grad(b)
    for copy in halo:
        copy.wait_recv()
    for b in edges:
        write_output(b, acc_x[b] + rest_forward(x_one, b))
    whole = total_of(early_map, map_count, early) * scale
    shifted = [pltpu.roll(whole, width - i * chan, 1)[:, :chan] if i else whole[:, :chan] for i in range(4)]
    filter_grad[0, :mid], filter_grad[0, mid:] = shifted[0], shifted[1]
    filter_grad[1, :mid], filter_grad[1, mid:] = shifted[2], shifted[3]
    for copy in adj:
        copy.wait_recv()
    for b in edges:
        write_grad(b)
    whole = total_of(late_map, map_count, late) * scale
    for i in range(4):
        lines = slice(i * quarter, (i + 1) * quarter)
        part = pltpu.roll(whole, width - i * chan, 1)[:, :chan] if i else whole[:, :chan]
        filter_grad[2, lines] = 2.0 * part - filter_grad[0, lines]
    for copy in sent:
        copy.wait_send()


def write(out, grad, filter_grad, out_hbm, grad_hbm, filter_grad_hbm, sems):
    copies = [
        pltpu.make_async_copy(out, out_hbm, sems.at[0]),
        pltpu.make_async_copy(grad, grad_hbm, sems.at[1]),
        pltpu.make_async_copy(filter_grad, filter_grad_hbm, sems.at[2]),
    ]
    for copy in copies:
        copy.start()
    for copy in copies:
        copy.wait()


def per_device(patch_count, map_count, maps, cotangent, tiles, columns, filters):
    copies, chan, pix = maps.shape
    nb, slots, bs, _ = tiles.shape
    rows = copies * chan
    order = filters.shape[0]
    scale = 1.0 / math.sqrt(copies * map_count * pix * patch_count)
    hbm = pl.BlockSpec(memory_space=pltpu.HBM)
    vmem = pl.BlockSpec(memory_space=pltpu.VMEM)
    dma = pltpu.SemaphoreType.DMA
    field = pltpu.VMEM((nb + 2 * REACH, rows, bs), BF16)
    own = pltpu.VMEM((nb, rows, bs), BF16)
    wide = pltpu.VMEM((nb, rows, bs), F32)
    rim = pltpu.VMEM((2, REACH, rows, bs), BF16)
    pin = lambda x: pltpu.with_memory_space_constraint(x, pltpu.HBM)
    results = (
        jax.ShapeDtypeStruct((rows, pix), BF16),
        jax.ShapeDtypeStruct((rows, pix), BF16),
        jax.ShapeDtypeStruct((order, chan, chan), F32),
    )
    held = pl.pallas_call(
        functools.partial(kernel, patch_count, map_count, copies, scale),
        out_shape=results,
        in_specs=[hbm, hbm, hbm, hbm, hbm],
        out_specs=(vmem, vmem, vmem),
        scratch_shapes=[
            pltpu.SMEM((slots, nb), jnp.int32),
            pltpu.VMEM((order, chan, chan), BF16),
            pltpu.VMEM((nb, slots, bs, bs), BF16),
            pltpu.VMEM((nb, slots, bs, bs), BF16),
            field,
            field,
            own,
            own,
            wide,
            wide,
            rim,
            rim,
            rim,
            rim,
            pltpu.VMEM((patch_count, chan // 2, 2 * rows), F32),
            pltpu.VMEM((map_count, chan // 2, 2 * rows), F32),
            pltpu.VMEM((patch_count, chan // 4, 2 * rows), F32),
            pltpu.VMEM((map_count, chan // 4, 2 * rows), F32),
            pltpu.VMEM((rows, 4 * rows), BF16),
            pltpu.VMEM((rows, 4 * rows), BF16),
            dma,
            dma,
            dma((nb,)),
            dma((nb,)),
            dma((nb,)),
            dma((2, 2)),
            dma((2, 2)),
            dma((2, 2)),
            dma((2, 2)),
            dma((2, patch_count - 1)),
            dma((2, patch_count - 1)),
            dma((2, map_count - 1)),
            dma((2, map_count - 1)),
        ],
        compiler_params=pltpu.CompilerParams(
            collective_id=0, has_side_effects=True, vmem_limit_bytes=40 * 1024 * 1024
        ),
    )(
        pin(maps.reshape(rows, pix)), pin(cotangent.reshape(rows, pix)), pin(tiles), pin(columns.T), pin(filters)
    )
    out, grad, filter_grad = pl.pallas_call(
        write,
        out_shape=results,
        in_specs=[vmem] * 3,
        out_specs=(hbm,) * 3,
        scratch_shapes=[dma((3,))],
        compiler_params=pltpu.CompilerParams(vmem_limit_bytes=4 * 1024 * 1024),
    )(*held)
    return out.reshape(copies, chan, pix), grad.reshape(copies, chan, pix), filter_grad


def solution(mesh):
    field = P("map", None, "patch")
    return jax.shard_map(
        functools.partial(per_device, mesh.shape["patch"], mesh.shape["map"]),
        mesh=mesh,
        in_specs=(field, field, P("patch", None, None, None), P("patch", None), P()),
        out_specs=(field, field, P()),
        check_vma=False,
    )
```
